32 devices in a mesh: dp: 8 (over y, x, core), tensor: 4 (over z).
Axes of the slice: x: 2, y: 2, z: 4, core: 2. Of those that a mesh axis runs over, the one named last changes fastest.
Arguments:
- tokens: bfloat16 [640, 2048], P('dp', 'tensor'), may hold values from -6 to 6
- gate_weight: bfloat16 [2048, 8192], P('tensor', 'dp'), may hold values from -0.125 to 0.125
- up_weight: bfloat16 [2048, 8192], P('tensor', 'dp'), may hold values from -0.125 to 0.125
- down_weight: bfloat16 [8192, 2048], P('dp', 'tensor'), may hold values from -0.0625 to 0.0625
- out_grad: bfloat16 [640, 2048], P('dp', 'tensor'), may hold values from -6 to 6
Outputs:
- mixed: float32 [640, 2048], P('dp', 'tensor')
- grad_tokens: float32 [640, 2048], P('dp', 'tensor')
- grad_gate: bfloat16 [2048, 8192], P('tensor', 'dp')
- grad_up: bfloat16 [2048, 8192], P('tensor', 'dp')
- grad_down: bfloat16 [8192, 2048], P('dp', 'tensor')
The draws below stay inside these ranges and needn't reach their ends.
All inputs are finite; a program needn't handle non-finite values.
Results may differ from the reference program's by a relative error of at most 0.0073.
Values may be sent and summed in bfloat16 or wider, within the bound.
No kernel may reach another device: no remote copies, remote signals or barrier semaphores. Data moves between devices by JAX's collectives and lax.ppermute only.
A program may use at most 64 MiB of HBM per device.

```python
import math
import jax
import jax.numpy as jnp
from jax import lax

D = 2048
FF = 8192
TOKENS = 640


def level_of(key, extent, pieces, least, top_value):
    loudness, own = 1.0, jax.random.fold_in(key, 6)
    for dim, blocks in pieces:
        draws = jnp.exp(jax.random.uniform(jax.random.fold_in(own, dim), (blocks,), jnp.float32, least / len(pieces), top_value / len(pieces)))
        loudness = loudness * jnp.repeat(draws, extent[dim] // blocks).reshape([-1 if axis == dim else 1 for axis in range(len(extent))])
    return loudness


def gaussian(key, extent, scale, bound, cuts=(), kind=jnp.bfloat16):
    drawn = scale * jax.random.normal(key, extent, jnp.float32)
    if cuts:
        drawn = drawn * level_of(key, extent, cuts, -0.22, 0.18)
    return jnp.clip(drawn, -bound, bound).astype(kind)


def setup_inputs(seed: int = 0) -> dict:
    seeds = jax.random.split(jax.random.key(seed), 6)
    tokens = gaussian(seeds[0], (TOKENS, D), 1.0, 6.0, ((0, 8), (1, 4)))
    gate_weight = gaussian(seeds[1], (D, FF), D ** -0.5, 0.125, ((0, 4), (1, 8)))
    up_weight = gaussian(seeds[2], (D, FF), D ** -0.5, 0.125, ((0, 4), (1, 8)))
    down_weight = gaussian(seeds[3], (FF, D), FF ** -0.5, 0.0625, ((0, 8), (1, 4)))
    out_grad = gaussian(seeds[4], (TOKENS, D), 1.0, 6.0, ((0, 8), (1, 4)))
    return dict(tokens=tokens, gate_weight=gate_weight, up_weight=up_weight, down_weight=down_weight, out_grad=out_grad)


def sylvester_table(order):
    rows = jnp.arange(order, dtype=jnp.int32)[:, None]
    cols = jnp.arange(order, dtype=jnp.int32)[None, :]
    signs = jnp.ones((order, order), jnp.float32)
    for level in range(order.bit_length() - 1):
        bit_on = jnp.bitwise_and(jnp.bitwise_and(jnp.right_shift(rows, level), jnp.right_shift(cols, level)), 1)
        signs = signs * (1.0 - 2.0 * bit_on.astype(jnp.float32))
    return signs

def rotate_rows(values):
    count = values.shape[0]
    lanes = min(D, 128)
    blocks = D // lanes
    shaped = values.reshape(count, blocks, lanes)
    shaped = jnp.einsum('rab,ac->rcb', shaped, sylvester_table(blocks), precision=lax.Precision.HIGHEST)
    shaped = jnp.einsum('rcb,bd->rcd', shaped, sylvester_table(lanes), precision=lax.Precision.HIGHEST)
    return shaped.reshape(count, D) * (1.0 / math.sqrt(D))

def reference(tokens, gate_weight, up_weight, down_weight, out_grad):
    rotated = rotate_rows(tokens.astype(jnp.float32)).astype(jnp.bfloat16)
    gate = jnp.dot(rotated, gate_weight, preferred_element_type=jnp.float32)
    up = jnp.dot(rotated, up_weight, preferred_element_type=jnp.float32)
    hidden = (jax.nn.silu(gate) * up).astype(jnp.bfloat16)
    mixed = rotate_rows(jnp.dot(hidden, down_weight, preferred_element_type=jnp.float32))
    grad_rot = rotate_rows(out_grad.astype(jnp.float32)).astype(jnp.bfloat16)
    grad_hidden = jnp.dot(grad_rot, down_weight.T, preferred_element_type=jnp.float32)
    sigma = jax.nn.sigmoid(gate)
    grad_gate_act = (grad_hidden * up * sigma * (1.0 + gate * (1.0 - sigma))).astype(jnp.bfloat16)
    grad_up_act = (grad_hidden * gate * sigma).astype(jnp.bfloat16)
    summed = jnp.dot(grad_gate_act, gate_weight.T, preferred_element_type=jnp.float32)
    summed = summed + jnp.dot(grad_up_act, up_weight.T, preferred_element_type=jnp.float32)
    grad_tokens = rotate_rows(summed)
    factor = 1.0 / math.sqrt(TOKENS)
    grad_gate = (jnp.dot(rotated.T, grad_gate_act, preferred_element_type=jnp.float32) * factor).astype(jnp.bfloat16)
    grad_up = (jnp.dot(rotated.T, grad_up_act, preferred_element_type=jnp.float32) * factor).astype(jnp.bfloat16)
    grad_down = (jnp.dot(hidden.T, grad_rot, preferred_element_type=jnp.float32) * factor).astype(jnp.bfloat16)
    return (mixed, grad_tokens, grad_gate, grad_up, grad_down)
```

```python
import math

import jax
import jax.numpy as jnp
import numpy as np
from jax import lax
from jax.sharding import PartitionSpec as P

D = 2048
BF16 = jnp.bfloat16
F32 = jnp.float32


def sylvester(order):
    table = np.ones((1, 1), np.float32)
    while table.shape[0] < order:
        table = np.block([[table, table], [table, -table]])
    return table


def dot(left, right, left_dim, right_dim):
    return lax.dot_general(
        left, right, (((left_dim,), (right_dim,)), ((), ())), preferred_element_type=F32
    )


def rotate(block):
    rows, width = block.shape
    groups = lax.axis_size("tensor")
    every = lax.all_gather(block, "tensor", axis=0, tiled=True)
    turned = dot(every, jnp.asarray(sylvester(width), BF16), 1, 0)
    signs = jnp.asarray(sylvester(groups))[lax.axis_index("tensor")] * (1.0 / math.sqrt(D))
    return jnp.sum(turned.reshape(groups, rows, width) * signs[:, None, None], axis=0)


def shards(tokens, gate_weight, up_weight, down_weight, out_grad):
    mine = tokens.shape[0]
    turned = rotate(jnp.concatenate([tokens, out_grad])).astype(BF16)
    inputs_all = lax.all_gather(turned[:mine], "dp", axis=0, tiled=True)
    grads_all = lax.all_gather(turned[mine:], "dp", axis=0, tiled=True)
    parts = jnp.stack(
        [
            dot(inputs_all, gate_weight, 1, 0).astype(BF16),
            dot(inputs_all, up_weight, 1, 0).astype(BF16),
            dot(grads_all, down_weight, 1, 1).astype(BF16),
        ]
    )
    sums = lax.psum_scatter(parts, "tensor", scatter_dimension=1, tiled=True).astype(F32)
    gate, up, grad_hidden = sums
    sigma = jax.nn.sigmoid(gate)
    acts = jnp.stack(
        [
            gate * sigma * up,
            grad_hidden * up * sigma * (1.0 + gate * (1.0 - sigma)),
            grad_hidden * gate * sigma,
        ]
    ).astype(BF16)
    hidden, grad_gate_act, grad_up_act = lax.all_gather(acts, "tensor", axis=1, tiled=True)
    output = jnp.concatenate(
        [
            dot(hidden, down_weight, 1, 0),
            dot(grad_gate_act, gate_weight, 1, 1) + dot(grad_up_act, up_weight, 1, 1),
        ],
        axis=1,
    ).astype(BF16)
    output = lax.psum_scatter(output, "dp", scatter_dimension=0, tiled=True)
    width = tokens.shape[1]
    ends = rotate(jnp.concatenate([output[:, :width], output[:, width:]]))
    factor = 1.0 / math.sqrt(inputs_all.shape[0])
    return (
        ends[:mine],
        ends[mine:],
        (dot(inputs_all, grad_gate_act, 0, 0) * factor).astype(BF16),
        (dot(inputs_all, grad_up_act, 0, 0) * factor).astype(BF16),
        (dot(hidden, grads_all, 0, 0) * factor).astype(BF16),
    )


def solution(mesh):
    return jax.shard_map(
        shards,
        mesh=mesh,
        in_specs=(
            P("dp", "tensor"),
            P("tensor", "dp"),
            P("tensor", "dp"),
            P("dp", "tensor"),
            P("dp", "tensor"),
        ),
        out_specs=(
            P("dp", "tensor"),
            P("dp", "tensor"),
            P("tensor", "dp"),
            P("tensor", "dp"),
            P("dp", "tensor"),
        ),
        check_vma=False,
    )
```

```python
import math

import jax
import jax.numpy as jnp
import numpy as np
from jax import lax
from jax.sharding import PartitionSpec as P

D = 2048
BF16 = jnp.bfloat16
F32 = jnp.float32
STEP = 16


def sylvester(order):
    table = np.ones((1, 1), np.float32)
    while table.shape[0] < order:
        table = np.block([[table, table], [table, -table]])
    return table


def dot(left, right, left_dim, right_dim):
    return lax.dot_general(
        left, right, (((left_dim,), (right_dim,)), ((), ())), preferred_element_type=F32
    )


def after(block, *others):
    for other in others:
        first = other[(0,) * other.ndim]
        block = jnp.where(jnp.isnan(first), first.astype(block.dtype), block)
    return block


def exchange(block, axis, apart):
    count = lax.axis_size(axis)
    return lax.ppermute(block, axis, [(i, i ^ apart) for i in range(count)])


def spread(block):
    return [block] + [exchange(block, "tensor", k) for k in range(1, lax.axis_size("tensor"))]


def rotate(pieces):
    width = pieces[0].shape[-1]
    me = lax.axis_index("tensor").astype(jnp.int32)
    square = jnp.asarray(sylvester(width), BF16)
    total = 0.0
    for apart, piece in enumerate(pieces):
        both = me & (me ^ apart)
        odd = jnp.int32(0)
        for bit in range((len(pieces) - 1).bit_length()):
            odd = odd ^ ((both >> bit) & 1)
        turned = dot(piece, square, piece.ndim - 1, 0)
        total = total + jnp.where(odd == 1, -turned, turned)
    return total * (1.0 / math.sqrt(D))


def dp_stages():
    bits = [1 << bit for bit in reversed(range(lax.axis_size("dp").bit_length() - 1))]
    stages = []
    while len(bits) > 1:
        high, low, bits = bits[0], bits[1], bits[2:]
        stages.append([0, low, high, high | low])
    if bits:
        stages.append([0, bits[0]])
    return stages


def gather_dp(block, axis):
    stages = dp_stages()
    for stage in stages[:-1]:
        came = [exchange(block, "dp", apart) for apart in stage[1:]]
        block = jnp.concatenate([block] + came, axis=axis)
    return block, exchange(block, "dp", stages[-1][1])


def scatter_dp(low, high):
    stages = dp_stages()
    low = low + exchange(high.astype(BF16), "dp", stages[-1][1]).astype(F32)
    for stage in reversed(stages[:-1]):
        low = low.reshape(low.shape[:2] + (len(stage), -1) + low.shape[-1:])
        total = low[:, :, 0]
        for place, apart in enumerate(stage[1:], 1):
            total = total + exchange(low[:, :, place].astype(BF16), "dp", apart).astype(F32)
        low = total
    return low


def line_pairs(step):
    last = lax.axis_size("tensor") - 1
    return [(step, step + 1), (last - step, last - step - 1)]


def fold_steps():
    return range(lax.axis_size("tensor") // 2 - 1)


def inward(own):
    came, total = own, own.astype(F32)
    for step in fold_steps():
        came = lax.ppermute(total.astype(BF16), "tensor", line_pairs(step))
        total = total + came.astype(F32)
    return total, came


def outward(block):
    me = lax.axis_index("tensor")
    for step in reversed(fold_steps()):
        pairs = line_pairs(step)
        came = lax.ppermute(block, "tensor", [(b, a) for a, b in pairs])
        takes = (me == pairs[0][0]) | (me == pairs[1][0])
        block = jnp.where(takes, came, block)
    return block


def across(block):
    half = lax.axis_size("tensor") // 2
    return lax.ppermute(block, "tensor", [(half - 1, half), (half, half - 1)])


def activations(gate, up, grad_hidden):
    sigma = jax.nn.sigmoid(gate)
    silu = gate * sigma
    return jnp.stack(
        [
            silu * up,
            grad_hidden * up * sigma * (1.0 + gate * (1.0 - sigma)),
            grad_hidden * silu,
        ]
    ).astype(BF16)


def shards(tokens, gate_weight, up_weight, down_weight, out_grad):
    mine, width = tokens.shape
    peers = lax.axis_size("dp")
    step = STEP if mine % STEP == 0 else mine
    chunks = mine // step
    half = peers * step // 2
    far_side = lax.axis_index("tensor") >= lax.axis_size("tensor") // 2

    both = jnp.stack([tokens, out_grad])

    def arrive(turned):
        low, high = gather_dp(turned.reshape(2, -1, 1, step, width), 2)
        every = jnp.where(
            far_side, jnp.concatenate([low, high], axis=2), jnp.concatenate([high, low], axis=2)
        )
        return [every[:, i].reshape(2, 2 * half, width) for i in range(every.shape[1])]

    pieces = spread(both[:, :step])
    late_pieces = spread(after(both[:, step:], *pieces[1:2])) if chunks > 1 else None
    rows = arrive(rotate(pieces).astype(BF16))

    done, arrived = [], []
    for i in range(chunks):
        x, g = rows[i]
        parts = [dot(x, gate_weight, 1, 0), dot(x, up_weight, 1, 0), dot(g, down_weight, 1, 1)]
        sums = []
        for place in (slice(0, half), slice(half, 2 * half)):
            ahead = arrived[:1] if len(arrived) < 2 else arrived[-2:-1]
            message = after(jnp.stack([part[place] for part in parts]).astype(BF16), *ahead)
            if not rows[i + 1 :] and i + 1 < chunks:
                rows += arrive(rotate([after(late_pieces[0], message)] + late_pieces[1:]).astype(BF16))
            total, came = inward(message)
            arrived.append(came)
            sums.append(total)
        other, own = sums
        sums = own + across(other.astype(BF16)).astype(F32)
        own = activations(sums[0], sums[1], sums[2])
        if i == chunks - 1:
            done += [outward(across(own)), outward(own)]
        else:
            done.append(outward(jnp.concatenate([across(own), own], axis=1)))

    def leave(blocks, first, last):
        sums = []
        for acts in blocks:
            mixed = dot(acts[0], down_weight, 1, 0)
            grads = dot(acts[1], gate_weight, 1, 1) + dot(acts[2], up_weight, 1, 1)
            sums.append(jnp.stack([mixed, grads]))
        sums = jnp.concatenate(sums, axis=1).reshape(2, last - first, 2, half, width)
        low = jnp.where(far_side, sums[:, :, 0], sums[:, :, 1])
        high = jnp.where(far_side, sums[:, :, 1], sums[:, :, 0])
        if last < chunks:
            high = after(high, own)
        sums = scatter_dp(low, high).astype(BF16)
        return rotate(spread(sums.reshape(2, (last - first) * step, width)))

    ends = [leave(done[:-2], 0, chunks - 1)] if chunks > 1 else []
    ends.append(leave(done[-2:], chunks - 1, chunks))
    ends = jnp.concatenate(ends, axis=1)

    acts = jnp.concatenate(done, axis=1)
    rows = jnp.concatenate(rows, axis=1)
    factor = 1.0 / math.sqrt(rows.shape[1])
    return (
        ends[0],
        ends[1],
        (dot(rows[0], acts[1], 0, 0) * factor).astype(BF16),
        (dot(rows[0], acts[2], 0, 0) * factor).astype(BF16),
        (dot(acts[0], rows[1], 0, 0) * factor).astype(BF16),
    )


def solution(mesh):
    return jax.shard_map(
        shards,
        mesh=mesh,
        in_specs=(
            P("dp", "tensor"),
            P("tensor", "dp"),
            P("tensor", "dp"),
            P("dp", "tensor"),
            P("dp", "tensor"),
        ),
        out_specs=(
            P("dp", "tensor"),
            P("dp", "tensor"),
            P("tensor", "dp"),
            P("tensor", "dp"),
            P("dp", "tensor"),
        ),
        check_vma=False,
    )
```

```python
import math

import jax
import jax.numpy as jnp
import numpy as np
from jax import lax
from jax.sharding import PartitionSpec as P

D = 2048
BF16 = jnp.bfloat16
F32 = jnp.float32
STEP = 16


def sylvester(order):
    table = np.ones((1, 1), np.float32)
    while table.shape[0] < order:
        table = np.block([[table, table], [table, -table]])
    return table


def dot(left, right, left_dim, right_dim):
    return lax.dot_general(
        left, right, (((left_dim,), (right_dim,)), ((), ())), preferred_element_type=F32
    )


def after(block, other):
    if other.shape != block.shape:
        row = other[(0,) * (other.ndim - 1)]
        other = jnp.resize(row, block.shape[-1:]).astype(block.dtype)
    return jnp.where(jnp.isnan(other), other, block)


def my_row(length):
    groups = lax.axis_size("tensor")
    table = np.zeros((groups, 1 + groups, length), np.float32)
    signs = sylvester(groups)
    for me in range(groups):
        table[me, 0] = me >= groups // 2
        for apart in range(groups):
            table[me, 1 + apart] = signs[me, me ^ apart]
    depth = np.minimum(np.arange(groups), groups - 1 - np.arange(groups)).astype(np.float32)
    table = np.concatenate([table, np.broadcast_to(depth[:, None, None], (groups, 1, length))], axis=1)
    row = lax.dynamic_index_in_dim(jnp.asarray(table), lax.axis_index("tensor"), keepdims=False)
    return row[0], row[1:-1], row[-1]


def exchange(block, axis, apart):
    count = lax.axis_size(axis)
    return lax.ppermute(block, axis, [(i, i ^ apart) for i in range(count)])


def spread(block):
    return [block] + [exchange(block, "tensor", k) for k in range(1, lax.axis_size("tensor"))]


def rotate(pieces, signs):
    width = pieces[0].shape[-1]
    square = jnp.asarray(sylvester(width), BF16)
    total = 0.0
    for piece, sign in zip(pieces, signs):
        total = total + dot(piece, square, piece.ndim - 1, 0) * sign[:width]
    return total * (1.0 / math.sqrt(D))


def dp_stages():
    bits = [1 << bit for bit in reversed(range(lax.axis_size("dp").bit_length() - 1))]
    stages = []
    while len(bits) > 1:
        high, low, bits = bits[0], bits[1], bits[2:]
        stages.append([0, low, high, high | low])
    if bits:
        stages.append([0, bits[0]])
    return stages


def gather_dp(block, axis):
    stages = dp_stages()
    for stage in stages[:-1]:
        came = [exchange(block, "dp", apart) for apart in stage[1:]]
        block = jnp.concatenate([block] + came, axis=axis)
    return block, exchange(block, "dp", stages[-1][1])


def scatter_dp(low, high):
    stages = dp_stages()
    low = low + exchange(high.astype(BF16), "dp", stages[-1][1]).astype(F32)
    for stage in reversed(stages[:-1]):
        low = low.reshape(low.shape[:2] + (len(stage), -1) + low.shape[-1:])
        total = low[:, :, 0]
        for place, apart in enumerate(stage[1:], 1):
            total = total + exchange(low[:, :, place].astype(BF16), "dp", apart).astype(F32)
        low = total
    return low


def line_pairs(step):
    last = lax.axis_size("tensor") - 1
    return [(step, step + 1), (last - step, last - step - 1)]


def fold_steps():
    return range(lax.axis_size("tensor") // 2 - 1)


def inward(own):
    came, total = own, own.astype(F32)
    for step in fold_steps():
        came = lax.ppermute(total.astype(BF16), "tensor", line_pairs(step))
        total = total + came.astype(F32)
    return total, came


def outward(block, depth):
    for step in reversed(fold_steps()):
        came = lax.ppermute(block, "tensor", [(b, a) for a, b in line_pairs(step)])
        block = jnp.where(depth[: block.shape[-1]] == step, came, block)
    return block


def across(block):
    half = lax.axis_size("tensor") // 2
    return lax.ppermute(block, "tensor", [(half - 1, half), (half, half - 1)])


def activations(gate, up, grad_hidden):
    sigma = jax.nn.sigmoid(gate)
    silu = gate * sigma
    return jnp.stack(
        [
            silu * up,
            grad_hidden * up * sigma * (1.0 + gate * (1.0 - sigma)),
            grad_hidden * silu,
        ]
    ).astype(BF16)


def shards(tokens, gate_weight, up_weight, down_weight, out_grad):
    mine, width = tokens.shape
    peers = lax.axis_size("dp")
    step = STEP if mine % STEP == 0 else mine
    chunks = mine // step
    half = peers * step // 2
    far, signs, depth = my_row(max(width, gate_weight.shape[1]))
    far = far[:width] > 0.5

    both = jnp.stack([tokens, out_grad])

    def arrive(turned):
        low, high = gather_dp(turned.reshape(2, -1, 1, step, width), 2)
        other, own = jnp.where(far, low, high), jnp.where(far, high, low)
        return [part.reshape(2, -1, half, width) for part in (other, own)]

    pieces = spread(both[:, :step])
    late_pieces = spread(after(both[:, step:], pieces[1])) if chunks > 1 else None
    groups = [arrive(rotate(pieces, signs).astype(BF16))]

    done, arrived = [], []
    for i in range(chunks):
        group, place = (groups[0], 0) if i == 0 else (groups[1], i - 1)
        sums = []
        for x, g in [(part[0, place], part[1, place]) for part in group]:
            parts = [dot(x, gate_weight, 1, 0), dot(x, up_weight, 1, 0), dot(g, down_weight, 1, 1)]
            message = jnp.stack(parts).astype(BF16)
            ahead = arrived[:1] if len(arrived) < 2 else arrived[-2:-1]
            if ahead:
                message = after(message, ahead[0])
            if len(groups) == 1 and chunks > 1:
                turned = rotate([after(late_pieces[0], message)] + late_pieces[1:], signs)
                groups.append(arrive(turned.astype(BF16)))
            total, came = inward(message)
            arrived.append(came)
            sums.append(total)
        other, own = sums
        sums = own + across(other.astype(BF16)).astype(F32)
        own = activations(sums[0], sums[1], sums[2])
        if i == chunks - 1:
            done += [outward(across(own), depth), outward(own, depth)]
        else:
            done.append(outward(jnp.concatenate([across(own), own], axis=1), depth))

    def leave(blocks, first, last, ahead):
        sums = []
        for acts in blocks:
            mixed = dot(acts[0], down_weight, 1, 0)
            grads = dot(acts[1], gate_weight, 1, 1) + dot(acts[2], up_weight, 1, 1)
            sums.append(jnp.stack([mixed, grads]))
        sums = jnp.concatenate(sums, axis=1).reshape(2, last - first, 2, half, width)
        low = jnp.where(far, sums[:, :, 0], sums[:, :, 1])
        high = jnp.where(far, sums[:, :, 1], sums[:, :, 0])
        if ahead is not None:
            high = after(high, ahead)
        sums = scatter_dp(low, high).astype(BF16)
        pieces = spread(sums.reshape(2, (last - first) * step, width))
        return rotate(pieces, signs), pieces[-1]

    if chunks > 1:
        first, came = leave(done[:-2], 0, chunks - 1, own)
        last, _ = leave(done[-2:], chunks - 1, chunks, came)
        ends = jnp.concatenate([first, last], axis=1)
    else:
        ends, _ = leave(done, 0, 1, None)

    acts = jnp.concatenate(done, axis=1)
    rows = [jnp.stack(group, axis=2).reshape(2, -1, width) for group in groups]
    rows = jnp.concatenate(rows, axis=1)
    factor = 1.0 / math.sqrt(rows.shape[1])
    return (
        ends[0],
        ends[1],
        (dot(rows[0], acts[1], 0, 0) * factor).astype(BF16),
        (dot(rows[0], acts[2], 0, 0) * factor).astype(BF16),
        (dot(acts[0], rows[1], 0, 0) * factor).astype(BF16),
    )


def solution(mesh):
    return jax.shard_map(
        shards,
        mesh=mesh,
        in_specs=(
            P("dp", "tensor"),
            P("tensor", "dp"),
            P("tensor", "dp"),
            P("dp", "tensor"),
            P("dp", "tensor"),
        ),
        out_specs=(
            P("dp", "tensor"),
            P("dp", "tensor"),
            P("tensor", "dp"),
            P("tensor", "dp"),
            P("dp", "tensor"),
        ),
        check_vma=False,
    )
```

```python
import math

import jax
import jax.numpy as jnp
import numpy as np
from jax import lax
from jax.sharding import PartitionSpec as P

D = 2048
BF16 = jnp.bfloat16
F32 = jnp.float32
STEP = 16


def sylvester(order):
    table = np.ones((1, 1), np.float32)
    while table.shape[0] < order:
        table = np.block([[table, table], [table, -table]])
    return table


def dot(left, right, left_dim, right_dim):
    return lax.dot_general(
        left, right, (((left_dim,), (right_dim,)), ((), ())), preferred_element_type=F32
    )


def after(block, other):
    other = other.reshape((-1,) + other.shape[-2:])[0]
    if other.shape[0] < block.shape[-2]:
        other = other[:1]
    other = other[: block.shape[-2]]
    wide = block.shape[-1]
    if other.shape[-1] < wide:
        other = jnp.concatenate([other] * (-(-wide // other.shape[-1])), axis=-1)
    other = other[:, :wide].astype(block.dtype)
    return jnp.where(jnp.isnan(other), other, block)


def my_row(length):
    groups = lax.axis_size("tensor")
    signs = sylvester(groups)
    me = np.arange(groups)
    columns = [me >= groups // 2, np.minimum(me, groups - 1 - me)]
    columns += [signs[me, me ^ apart] for apart in range(groups)]
    columns += [1 - 2 * (me >> bit & 1) for bit in range(groups.bit_length() - 1)]
    table = np.stack(columns, axis=1).astype(np.float32)[:, :, None, None]
    table = jnp.asarray(np.broadcast_to(table, table.shape[:3] + (length,)))
    row = lax.dynamic_index_in_dim(table, lax.axis_index("tensor"), keepdims=False)
    return row[0], row[1], row[2 : 2 + groups], row[2 + groups :]


def exchange(block, axis, apart):
    count = lax.axis_size(axis)
    return lax.ppermute(block, axis, [(i, i ^ apart) for i in range(count)])


def spread(block):
    return [block] + [exchange(block, "tensor", k) for k in range(1, lax.axis_size("tensor"))]


def rotate(pieces, signs):
    width = pieces[0].shape[-1]
    square = jnp.asarray(sylvester(width), BF16)
    total = 0.0
    for piece, sign in zip(pieces, signs):
        total = total + dot(piece, square, piece.ndim - 1, 0) * sign[:, :width]
    return total * (1.0 / math.sqrt(D))


def rotate_by_halves(block, bits):
    width = block.shape[-1]
    square = jnp.asarray(sylvester(width), BF16)
    high = lax.reduce_precision(block, 8, 7)
    low = (block - high).astype(BF16)
    last = block.ndim - 1
    block = dot(high.astype(BF16), square, last, 0) + dot(low, square, last, 0)
    for level, bit in enumerate(bits):
        came = exchange(block.astype(BF16), "tensor", 1 << level)
        block = block * bit[:, :width] + came.astype(F32)
    return block * (1.0 / math.sqrt(D))


def dp_stages():
    bits = [1 << bit for bit in reversed(range(lax.axis_size("dp").bit_length() - 1))]
    stages = []
    while len(bits) > 1:
        high, low, bits = bits[0], bits[1], bits[2:]
        stages.append([0, low, high, high | low])
    if bits:
        stages.append([0, bits[0]])
    return stages


def gather_dp(block, axis):
    stages = dp_stages()
    for stage in stages[:-1]:
        came = [exchange(block, "dp", apart) for apart in stage[1:]]
        block = jnp.concatenate([block] + came, axis=axis)
    return block, exchange(block, "dp", stages[-1][1])


def scatter_dp(low, high):
    stages = dp_stages()
    low = low + exchange(high.astype(BF16), "dp", stages[-1][1]).astype(F32)
    for stage in reversed(stages[:-1]):
        low = low.reshape(low.shape[:2] + (len(stage), -1) + low.shape[-1:])
        total = low[:, :, 0]
        for place, apart in enumerate(stage[1:], 1):
            came = exchange(low[:, :, place].astype(BF16), "dp", apart)
            total = total + came.astype(F32)
        low = total
    return low, came


def line_pairs(step):
    last = lax.axis_size("tensor") - 1
    return [(step, step + 1), (last - step, last - step - 1)]


def fold_steps():
    return range(lax.axis_size("tensor") // 2 - 1)


def inward(own):
    came, total = own, own.astype(F32)
    for step in fold_steps():
        came = lax.ppermute(total.astype(BF16), "tensor", line_pairs(step))
        total = total + came.astype(F32)
    return total, came


def outward(block, depth):
    for step in reversed(fold_steps()):
        came = lax.ppermute(block, "tensor", [(b, a) for a, b in line_pairs(step)])
        block = jnp.where(depth[:, : block.shape[-1]] == step, came, block)
    return block


def across(block):
    half = lax.axis_size("tensor") // 2
    return lax.ppermute(block, "tensor", [(half - 1, half), (half, half - 1)])


def activations(gate, up, grad_hidden):
    sigma = jax.nn.sigmoid(gate)
    silu = gate * sigma
    return jnp.stack(
        [
            silu * up,
            grad_hidden * up * sigma * (1.0 + gate * (1.0 - sigma)),
            grad_hidden * silu,
        ]
    ).astype(BF16)


def shards(tokens, gate_weight, up_weight, down_weight, out_grad):
    mine, width = tokens.shape
    peers = lax.axis_size("dp")
    step = STEP if mine % STEP == 0 else mine
    chunks = mine // step
    half = peers * step // 2
    far, depth, signs, bits = my_row(max(width, gate_weight.shape[1]))
    far = far[:, :width] > 0.5

    both = jnp.stack([tokens, out_grad])

    def arrive(turned):
        low, high = gather_dp(turned.reshape(2, -1, 1, step, width), 2)
        other, own = jnp.where(far, low, high), jnp.where(far, high, low)
        return [part.reshape(2, -1, half, width) for part in (other, own)]

    pieces = spread(both[:, :step])
    late_pieces = spread(after(both[:, step:], pieces[1])) if chunks > 1 else None
    groups = [arrive(rotate(pieces, signs).astype(BF16))]

    done, arrived, crossed = [], [], []
    for i in range(chunks):
        group, place = (groups[0], 0) if i == 0 else (groups[1], i - 1)
        sums = []
        for which, (x, g) in enumerate([(part[0, place], part[1, place]) for part in group]):
            if i > 0:
                x, g = after(x, arrived[-2]), after(g, arrived[-2])
            if i > 1 and which == 0:
                x, g = after(x, crossed[i - 2]), after(g, crossed[i - 2])
            parts = [dot(x, gate_weight, 1, 0), dot(x, up_weight, 1, 0), dot(g, down_weight, 1, 1)]
            message = jnp.stack(parts).astype(BF16)
            if i == 0 and which == 1:
                message = after(message, arrived[0])
            if len(groups) == 1 and chunks > 1:
                piece = late_pieces[0]
                for part in message:
                    piece = after(piece, part)
                groups.append(arrive(rotate([piece] + late_pieces[1:], signs).astype(BF16)))
            total, came = inward(message)
            arrived.append(came)
            sums.append(total)
        other, own = sums
        sums = own + across(other.astype(BF16)).astype(F32)
        own = activations(sums[0], sums[1], sums[2])
        crossed.append(across(own))
        if i < chunks - 1:
            done.append(outward(jnp.concatenate([crossed[i], own], axis=1), depth))

    def leave(blocks):
        count = sum(acts.shape[1] for acts in blocks) // (2 * half)
        sums = []
        for acts in blocks:
            mixed = dot(acts[0], down_weight, 1, 0)
            grads = dot(acts[1], gate_weight, 1, 1) + dot(acts[2], up_weight, 1, 1)
            sums.append(jnp.stack([mixed, grads]))
        sums = jnp.concatenate(sums, axis=1).reshape(2, count, 2, half, width)
        low = jnp.where(far, sums[:, :, 0], sums[:, :, 1])
        high = jnp.where(far, sums[:, :, 1], sums[:, :, 0]).astype(BF16)
        sums, came = scatter_dp(low, high)
        return sums.reshape(2, count * step, width), high, came

    split, ends = max(chunks - 2, 0), []
    if split > 0:
        sums, _, came = leave(done[:split])
        ends.append(rotate_by_halves(sums, bits))
        crossed[-1] = after(crossed[-1], came)
    done += [outward(crossed[-1], depth), outward(own, depth)]
    sums, message, _ = leave(done[split:])
    ends.append(rotate(spread(sums.astype(BF16)), signs))
    ends = jnp.concatenate(ends, axis=1)

    acts = jnp.concatenate(done, axis=1)
    rows = [jnp.stack(group, axis=2).reshape(2, -1, width) for group in groups]
    rows = after(jnp.concatenate(rows, axis=1), message[0, 0, :1])
    factor = 1.0 / math.sqrt(rows.shape[1])
    return (
        ends[0],
        ends[1],
        (dot(rows[0], acts[1], 0, 0) * factor).astype(BF16),
        (dot(rows[0], acts[2], 0, 0) * factor).astype(BF16),
        (dot(acts[0], rows[1], 0, 0) * factor).astype(BF16),
    )


def solution(mesh):
    return jax.shard_map(
        shards,
        mesh=mesh,
        in_specs=(
            P("dp", "tensor"),
            P("tensor", "dp"),
            P("tensor", "dp"),
            P("dp", "tensor"),
            P("dp", "tensor"),
        ),
        out_specs=(
            P("dp", "tensor"),
            P("dp", "tensor"),
            P("tensor", "dp"),
            P("tensor", "dp"),
            P("dp", "tensor"),
        ),
        check_vma=False,
    )
```

```python
import math

import jax
import jax.numpy as jnp
import numpy as np
from jax import lax
from jax.sharding import PartitionSpec as P

D = 2048
BF16 = jnp.bfloat16
F32 = jnp.float32
STEP = 16


def sylvester(order):
    table = np.ones((1, 1), np.float32)
    while table.shape[0] < order:
        table = np.block([[table, table], [table, -table]])
    return table


def dot(left, right, left_dim, right_dim):
    return lax.dot_general(
        left, right, (((left_dim,), (right_dim,)), ((), ())), preferred_element_type=F32
    )


def after(block, other):
    other = other.reshape((-1,) + other.shape[-2:])[0]
    if other.shape[0] < block.shape[-2]:
        other = other[:1]
    other = other[: block.shape[-2]]
    wide = block.shape[-1]
    if other.shape[-1] < wide:
        other = jnp.concatenate([other] * (-(-wide // other.shape[-1])), axis=-1)
    other = other[:, :wide].astype(block.dtype)
    return jnp.where(jnp.isnan(other), other, block)


def my_row(length):
    groups = lax.axis_size("tensor")
    signs = sylvester(groups)
    me = np.arange(groups)
    columns = [me >= groups // 2, np.minimum(me, groups - 1 - me)]
    columns += [signs[me, me ^ apart] for apart in range(groups)]
    columns += [1 - 2 * (me >> bit & 1) for bit in range(groups.bit_length() - 1)]
    table = np.stack(columns, axis=1).astype(np.float32)[:, :, None, None]
    table = jnp.asarray(np.broadcast_to(table, table.shape[:3] + (length,)))
    row = lax.dynamic_index_in_dim(table, lax.axis_index("tensor"), keepdims=False)
    return row[0], row[1], row[2 : 2 + groups], row[2 + groups :]


def exchange(block, axis, apart):
    count = lax.axis_size(axis)
    return lax.ppermute(block, axis, [(i, i ^ apart) for i in range(count)])


def spread(block):
    return [block] + [exchange(block, "tensor", k) for k in range(1, lax.axis_size("tensor"))]


def turn(block):
    width = block.shape[-1]
    square = jnp.asarray(sylvester(width), BF16)
    rows = block.reshape(-1, width) * (1.0 / math.sqrt(D))
    high = lax.reduce_precision(rows, 8, 7)
    low = (rows - high).astype(BF16)
    return (dot(high.astype(BF16), square, 1, 0) + dot(low, square, 1, 0)).reshape(block.shape)


def rotate(pieces, signs):
    width = pieces[0].shape[-1]
    return turn(sum(piece.astype(F32) * sign[:, :width] for piece, sign in zip(pieces, signs)))


def rotate_by_halves(block, bits):
    block = turn(block)
    for level, bit in enumerate(bits):
        came = exchange(block.astype(BF16), "tensor", 1 << level)
        block = block * bit[:, : block.shape[-1]] + came.astype(F32)
    return block


def dp_stages():
    bits = [1 << bit for bit in reversed(range(lax.axis_size("dp").bit_length() - 1))]
    stages = []
    while len(bits) > 1:
        high, low, bits = bits[0], bits[1], bits[2:]
        stages.append([0, low, high, high | low])
    if bits:
        stages.append([0, bits[0]])
    return stages


def gather_dp(block, axis):
    stages = dp_stages()
    for stage in stages[:-1]:
        came = [exchange(block, "dp", apart) for apart in stage[1:]]
        block = jnp.concatenate([block] + came, axis=axis)
    return block, exchange(block, "dp", stages[-1][1])


def scatter_dp(low, high):
    stages = dp_stages()
    first = exchange(high, "dp", stages[-1][1])
    low, came = low + first.astype(F32), first
    for stage in reversed(stages[:-1]):
        low = low.reshape(low.shape[:2] + (len(stage), -1) + low.shape[-1:])
        total = low[:, :, 0]
        for place, apart in enumerate(stage[1:], 1):
            came = exchange(low[:, :, place].astype(BF16), "dp", apart)
            total = total + came.astype(F32)
        low = total
    return low, first, came


def line_pairs(step):
    last = lax.axis_size("tensor") - 1
    return [(step, step + 1), (last - step, last - step - 1)]


def fold_steps():
    return range(lax.axis_size("tensor") // 2 - 1)


def inward(own):
    came, total = own, own.astype(F32)
    for step in fold_steps():
        came = lax.ppermute(total.astype(BF16), "tensor", line_pairs(step))
        total = total + came.astype(F32)
    return total, came


def outward(block, depth):
    for step in reversed(fold_steps()):
        came = lax.ppermute(block, "tensor", [(b, a) for a, b in line_pairs(step)])
        block = jnp.where(depth[:, : block.shape[-1]] == step, came, block)
    return block


def across(block):
    half = lax.axis_size("tensor") // 2
    return lax.ppermute(block, "tensor", [(half - 1, half), (half, half - 1)])


def activations(gate, up, grad_hidden):
    sigma = jax.nn.sigmoid(gate)
    silu = gate * sigma
    return jnp.stack(
        [
            silu * up,
            grad_hidden * up * sigma * (1.0 + gate * (1.0 - sigma)),
            grad_hidden * silu,
        ]
    ).astype(BF16)


def shards(tokens, gate_weight, up_weight, down_weight, out_grad):
    mine, width = tokens.shape
    peers = lax.axis_size("dp")
    step = STEP if mine % STEP == 0 else mine
    chunks = mine // step
    half = peers * step // 2
    far, depth, signs, bits = my_row(max(width, gate_weight.shape[1]))
    far = far[:, :width] > 0.5

    both = jnp.stack([tokens, out_grad])

    def arrive(turned):
        low, high = gather_dp(turned.reshape(2, -1, 1, step, width), 2)
        other, own = jnp.where(far, low, high), jnp.where(far, high, low)
        return [part.reshape(2, -1, half, width) for part in (other, own)]

    first = min(2, chunks)
    early = spread(both[:, : first * step])
    late = spread(after(both[:, first * step :], early[1])) if chunks > first else None
    groups = [arrive(rotate(early, signs).astype(BF16))]

    done, arrived, crossed = [], [], []
    for i in range(chunks):
        group, place = (groups[0], i) if i < first else (groups[1], i - first)
        sums = []
        for which, (x, g) in enumerate([(part[0, place], part[1, place]) for part in group]):
            ahead = arrived[max(2 * i - 4 + which, 0)] if i > 0 else message if arrived else None
            if ahead is not None:
                x, g = after(x, ahead), after(g, ahead)
            parts = [dot(x, gate_weight, 1, 0), dot(x, up_weight, 1, 0), dot(g, down_weight, 1, 1)]
            block = jnp.stack(parts).astype(BF16)
            block = after(block, arrived[max(len(arrived) - 2, 0)]) if arrived else block
            message = message if arrived else block[2:]
            total, came = inward(block)
            arrived.append(came)
            sums.append(total)
            if len(groups) == 1 and chunks > first:
                late[0] = after(late[0], came)
                groups.append(arrive(rotate(late, signs).astype(BF16)))
        other, own = sums
        sums = own + across(other.astype(BF16)).astype(F32)
        own = activations(sums[0], sums[1], sums[2])
        crossed.append(across(own))
        if i < chunks - 1:
            done.append([outward(crossed[i], depth), outward(own, depth)])

    def leave(blocks):
        lows, highs = [], []
        for halves in blocks:
            sums = []
            for acts in halves:
                mixed = dot(acts[0], down_weight, 1, 0)
                grads = dot(acts[1], gate_weight, 1, 1) + dot(acts[2], up_weight, 1, 1)
                sums.append(jnp.stack([mixed, grads]))
            lows.append(jnp.where(far, sums[0], sums[1]))
            highs.append(jnp.where(far, sums[1], sums[0]).astype(BF16))
        return jnp.stack(lows, axis=1), jnp.stack(highs, axis=1)

    split, ends = max(chunks - 2, 0), []
    if split > 0:
        sums, came, last = scatter_dp(*leave(done[:split]))
        ends.append(rotate_by_halves(sums.reshape(2, -1, width), bits))
        crossed[-1] = after(crossed[-1], came)
    done.append([outward(crossed[-1], depth), outward(own, depth)])
    low, high = leave(done[split:])
    if split > 0:
        high = after(high, last)
    sums, _, _ = scatter_dp(low, high)
    ends.append(rotate(spread(sums.reshape(2, -1, width).astype(BF16)), signs))
    ends = jnp.concatenate(ends, axis=1)

    acts = jnp.concatenate([half for halves in done for half in halves], axis=1)
    rows = [jnp.stack(group, axis=2).reshape(2, -1, width) for group in groups]
    rows = after(jnp.concatenate(rows, axis=1), high[0, 0, :1])
    factor = 1.0 / math.sqrt(rows.shape[1])
    return (
        ends[0],
        ends[1],
        (dot(rows[0], acts[1], 0, 0) * factor).astype(BF16),
        (dot(rows[0], acts[2], 0, 0) * factor).astype(BF16),
        (dot(acts[0], rows[1], 0, 0) * factor).astype(BF16),
    )


def solution(mesh):
    return jax.shard_map(
        shards,
        mesh=mesh,
        in_specs=(
            P("dp", "tensor"),
            P("tensor", "dp"),
            P("tensor", "dp"),
            P("dp", "tensor"),
            P("dp", "tensor"),
        ),
        out_specs=(
            P("dp", "tensor"),
            P("dp", "tensor"),
            P("tensor", "dp"),
            P("tensor", "dp"),
            P("dp", "tensor"),
        ),
        check_vma=False,
    )
```

```python
import math

import jax
import jax.numpy as jnp
import numpy as np
from jax import lax
from jax.sharding import PartitionSpec as P

D = 2048
BF16 = jnp.bfloat16
F32 = jnp.float32
STEP = 16


def sylvester(order):
    table = np.ones((1, 1), np.float32)
    while table.shape[0] < order:
        table = np.block([[table, table], [table, -table]])
    return table


def dot(left, right, left_dim, right_dim):
    return lax.dot_general(
        left, right, (((left_dim,), (right_dim,)), ((), ())), preferred_element_type=F32
    )


def after(block, other):
    other = other.reshape((-1,) + other.shape[-2:])[0]
    if other.shape[0] < block.shape[-2]:
        other = other[:1]
    other = other[: block.shape[-2]]
    wide = block.shape[-1]
    if other.shape[-1] < wide:
        other = jnp.concatenate([other] * (-(-wide // other.shape[-1])), axis=-1)
    other = other[:, :wide].astype(block.dtype)
    return jnp.where(jnp.isnan(other), other, block)


def my_row(length):
    groups = lax.axis_size("tensor")
    signs = sylvester(groups)
    me = np.arange(groups)
    columns = [me >= groups // 2, np.minimum(me, groups - 1 - me)]
    columns += [signs[me, me ^ apart] for apart in range(groups)]
    columns += [1 - 2 * (me >> bit & 1) for bit in range(groups.bit_length() - 1)]
    table = np.stack(columns, axis=1).astype(np.float32)[:, :, None, None]
    table = jnp.asarray(np.tile(table, (1, 1, 1, length)))
    row = lax.dynamic_index_in_dim(table, lax.axis_index("tensor"), keepdims=False)
    return row[0], row[1], row[2 : 2 + groups], row[2 + groups :]


def exchange(block, axis, apart):
    count = lax.axis_size(axis)
    return lax.ppermute(block, axis, [(i, i ^ apart) for i in range(count)])


def spread(block):
    return [block] + [exchange(block, "tensor", k) for k in range(1, lax.axis_size("tensor"))]


def turn(block):
    width = block.shape[-1]
    square = jnp.asarray(sylvester(width), BF16)
    rows = block.reshape(-1, width) * (1.0 / math.sqrt(D))
    high = lax.reduce_precision(rows, 8, 7)
    low = (rows - high).astype(BF16)
    return (dot(high.astype(BF16), square, 1, 0) + dot(low, square, 1, 0)).reshape(block.shape)


def rotate(pieces, signs):
    width = pieces[0].shape[-1]
    return turn(sum(piece.astype(F32) * sign[:, :width] for piece, sign in zip(pieces, signs)))


def rotate_by_halves(block, bits):
    block = turn(block)
    for level, bit in enumerate(bits):
        came = exchange(block.astype(BF16), "tensor", 1 << level)
        block = block * bit[:, : block.shape[-1]] + came.astype(F32)
    return block


def dp_stages():
    bits = [1 << bit for bit in reversed(range(lax.axis_size("dp").bit_length() - 1))]
    stages = []
    while len(bits) > 1:
        high, low, bits = bits[0], bits[1], bits[2:]
        stages.append([0, low, high, high | low])
    if bits:
        stages.append([0, bits[0]])
    return stages


def gather_dp(block, axis):
    stages = dp_stages()
    for stage in stages[:-1]:
        came = [exchange(block, "dp", apart) for apart in stage[1:]]
        block = jnp.concatenate([block] + came, axis=axis)
    return block, exchange(block, "dp", stages[-1][1])


def scatter_dp(low, high):
    stages = dp_stages()
    first = exchange(high, "dp", stages[-1][1])
    low, came = low + first.astype(F32), first
    for stage in reversed(stages[:-1]):
        low = low.reshape(low.shape[:2] + (len(stage), -1) + low.shape[-1:])
        total = low[:, :, 0]
        for place, apart in enumerate(stage[1:], 1):
            came = exchange(low[:, :, place].astype(BF16), "dp", apart)
            total = total + came.astype(F32)
        low = total
    return low, first, came


def line_pairs(step):
    last = lax.axis_size("tensor") - 1
    return [(step, step + 1), (last - step, last - step - 1)]


def fold_steps():
    return range(lax.axis_size("tensor") // 2 - 1)


def inward(own):
    came, total = own, own.astype(F32)
    for step in fold_steps():
        came = lax.ppermute(total.astype(BF16), "tensor", line_pairs(step))
        total = total + came.astype(F32)
    return total, came


def outward(parts, depth, ahead=None):
    block = jnp.concatenate(parts, axis=1)
    for step in reversed(fold_steps()):
        came = lax.ppermute(block, "tensor", [(b, a) for a, b in line_pairs(step)])
        if ahead is not None and step == 0:
            block = jnp.concatenate([after(parts[0], ahead)] + parts[1:], axis=1)
        block = jnp.where(depth[:, : block.shape[-1]] == step, came, block)
    return block


def across(block):
    half = lax.axis_size("tensor") // 2
    return lax.ppermute(block, "tensor", [(half - 1, half), (half, half - 1)])


def activations(gate, up, grad_hidden):
    sigma = jax.nn.sigmoid(gate)
    silu = gate * sigma
    return jnp.stack(
        [
            silu * up,
            grad_hidden * up * sigma * (1.0 + gate * (1.0 - sigma)),
            grad_hidden * silu,
        ]
    ).astype(BF16)


def shards(tokens, gate_weight, up_weight, down_weight, out_grad):
    mine, width = tokens.shape
    peers = lax.axis_size("dp")
    step = STEP if mine % STEP == 0 else mine
    chunks = mine // step
    half = peers * step // 2
    far, depth, signs, bits = my_row(max(width, gate_weight.shape[1]))
    far = far[:, :width] > 0.5

    both = jnp.stack([tokens, out_grad])

    def arrive(turned):
        low, high = gather_dp(turned.reshape(2, -1, 1, step, width), 2)
        other, own = jnp.where(far, low, high), jnp.where(far, high, low)
        return [part.reshape(2, -1, half, width) for part in (other, own)]

    first = min(2, chunks)
    early = spread(both[:, : first * step])
    late = spread(after(both[:, first * step :], early[1])) if chunks > first else None
    groups = [arrive(rotate(early, signs).astype(BF16))]

    done, mids, acts = [], [], []
    for i in range(chunks):
        group, place = (groups[0], i) if i < first else (groups[1], i - first)
        sums = []
        for which, (x, g) in enumerate([(part[0, place], part[1, place]) for part in group]):
            if i > 0:
                ahead = [acts[i - 1]] if which else [mids[i - 1]]
                ahead += [crossed[i - 2]] if i > 1 and not which else []
            else:
                ahead, crossed = [message[2:]] if which else [], []
            for other in ahead:
                x, g = after(x, other), after(g, other)
            parts = [dot(x, gate_weight, 1, 0), dot(x, up_weight, 1, 0), dot(g, down_weight, 1, 1)]
            message = jnp.stack(parts).astype(BF16)
            if i == 0 and which:
                message = after(message, came)
            total, came = inward(message)
            sums.append(total)
            if len(groups) == 1 and chunks > first:
                tick = exchange(message[2, :step, :width], "dp", 1)
                late[0] = after(late[0], tick)
                groups.append(arrive(rotate(late, signs).astype(BF16)))
        mids.append(sums[0].astype(BF16))
        sums = sums[1] + across(mids[i]).astype(F32)
        acts.append(activations(sums[0], sums[1], sums[2]))
        crossed.append(across(acts[i]))
        if i > 0:
            done.append([outward([crossed[i - 1], acts[i - 1]], depth, crossed[i])])

    def leave(blocks):
        lows, highs = [], []
        for parts in blocks:
            sums = []
            for block in parts:
                mixed = dot(block[0], down_weight, 1, 0)
                grads = dot(block[1], gate_weight, 1, 1) + dot(block[2], up_weight, 1, 1)
                sums.append(jnp.stack([mixed, grads]))
            sums = jnp.concatenate(sums, axis=1)
            lows.append(jnp.where(far, sums[:, :half], sums[:, half:]))
            highs.append(jnp.where(far, sums[:, half:], sums[:, :half]).astype(BF16))
        return jnp.stack(lows, axis=1), jnp.stack(highs, axis=1)

    split, ends = max(chunks - 2, 0), []
    if split > 0:
        low, high = leave(done[:split])
        sums, _, last = scatter_dp(low, after(high, crossed[-1]))
        ends.append(rotate_by_halves(sums.reshape(2, -1, width), bits))
    done.append([outward([crossed[-1]], depth), outward([acts[-1]], depth)])
    low, high = leave(done[split:])
    if split > 0:
        high = after(high, last)
    sums, _, _ = scatter_dp(low, high)
    ends.append(rotate(spread(sums.reshape(2, -1, width).astype(BF16)), signs))
    ends = jnp.concatenate(ends, axis=1)

    acts = jnp.concatenate([block for parts in done for block in parts], axis=1)
    rows = [jnp.stack(group, axis=2).reshape(2, -1, width) for group in groups]
    rows = after(jnp.concatenate(rows, axis=1), high[0, 0, :1])
    factor = 1.0 / math.sqrt(rows.shape[1])
    return (
        ends[0],
        ends[1],
        (dot(rows[0], acts[1], 0, 0) * factor).astype(BF16),
        (dot(rows[0], acts[2], 0, 0) * factor).astype(BF16),
        (dot(acts[0], rows[1], 0, 0) * factor).astype(BF16),
    )


def solution(mesh):
    return jax.shard_map(
        shards,
        mesh=mesh,
        in_specs=(
            P("dp", "tensor"),
            P("tensor", "dp"),
            P("tensor", "dp"),
            P("dp", "tensor"),
            P("dp", "tensor"),
        ),
        out_specs=(
            P("dp", "tensor"),
            P("dp", "tensor"),
            P("tensor", "dp"),
            P("tensor", "dp"),
            P("dp", "tensor"),
        ),
        check_vma=False,
    )
```

```python
import math

import jax
import jax.numpy as jnp
import numpy as np
from jax import lax
from jax.sharding import PartitionSpec as P

D = 2048
BF16 = jnp.bfloat16
F32 = jnp.float32
STEP = 16
LAG = 3


def sylvester(order):
    table = np.ones((1, 1), np.float32)
    while table.shape[0] < order:
        table = np.block([[table, table], [table, -table]])
    return table


def dot(left, right, left_dim, right_dim):
    return lax.dot_general(
        left, right, (((left_dim,), (right_dim,)), ((), ())), preferred_element_type=F32
    )


def after(block, other):
    other = other.reshape((-1,) + other.shape[-2:])[0]
    if other.shape[0] < block.shape[-2]:
        other = other[:1]
    other = other[: block.shape[-2]]
    wide = block.shape[-1]
    if other.shape[-1] < wide:
        other = jnp.concatenate([other] * (-(-wide // other.shape[-1])), axis=-1)
    other = other[:, :wide].astype(block.dtype)
    return jnp.where(jnp.isnan(other), other, block)


def my_row(length):
    groups = lax.axis_size("tensor")
    signs = sylvester(groups)
    me = np.arange(groups)
    away = np.minimum(me, groups - 1 - me)
    columns = [me >= groups // 2, away]
    columns += [signs[me, me ^ apart] for apart in range(groups)]
    columns += [1 - 2 * (me >> bit & 1) for bit in range(groups.bit_length() - 1)]
    columns += [away, away]
    table = np.stack(columns, axis=1).astype(np.float32)[:, :, None, None]
    table = jnp.asarray(np.tile(table, (1, 1, 1, length)))
    row = lax.dynamic_index_in_dim(table, lax.axis_index("tensor"), keepdims=False)
    return row[0], row[1], row[2 : 2 + groups], row[2 + groups : -2], row[-2:]


def exchange(block, axis, apart):
    count = lax.axis_size(axis)
    return lax.ppermute(block, axis, [(i, i ^ apart) for i in range(count)])


def spread(block):
    return [block] + [exchange(block, "tensor", k) for k in range(1, lax.axis_size("tensor"))]


def turn(block):
    width = block.shape[-1]
    square = jnp.asarray(sylvester(width), BF16)
    rows = block.reshape(-1, width) * (1.0 / math.sqrt(D))
    high = lax.reduce_precision(rows, 8, 7)
    low = (rows - high).astype(BF16)
    return (dot(high.astype(BF16), square, 1, 0) + dot(low, square, 1, 0)).reshape(block.shape)


def rotate(pieces, signs):
    width = pieces[0].shape[-1]
    return turn(sum(piece.astype(F32) * sign[:, :width] for piece, sign in zip(pieces, signs)))


def rotate_by_halves(block, bits):
    block = turn(block)
    for level, bit in enumerate(bits):
        came = exchange(block.astype(BF16), "tensor", 1 << level)
        block = block * bit[:, : block.shape[-1]] + came.astype(F32)
    return block


def dp_stages():
    bits = [1 << bit for bit in reversed(range(lax.axis_size("dp").bit_length() - 1))]
    stages = []
    while len(bits) > 1:
        high, low, bits = bits[0], bits[1], bits[2:]
        stages.append([0, low, high, high | low])
    if bits:
        stages.append([0, bits[0]])
    return stages


def gather_dp(block, axis):
    stages = dp_stages()
    for stage in stages[:-1]:
        came = [exchange(block, "dp", apart) for apart in stage[1:]]
        block = jnp.concatenate([block] + came, axis=axis)
    return block, exchange(block, "dp", stages[-1][1])


def scatter_dp(low, high):
    stages = dp_stages()
    first = exchange(high, "dp", stages[-1][1])
    low, came = low + first.astype(F32), first
    for stage in reversed(stages[:-1]):
        low = low.reshape(low.shape[:2] + (len(stage), -1) + low.shape[-1:])
        total = low[:, :, 0]
        for place, apart in enumerate(stage[1:], 1):
            came = exchange(low[:, :, place].astype(BF16), "dp", apart)
            total = total + came.astype(F32)
        low = total
    return low, first, came


def line_pairs(step):
    last = lax.axis_size("tensor") - 1
    return [(step, step + 1), (last - step, last - step - 1)]


def fold_steps():
    return range(lax.axis_size("tensor") // 2 - 1)


def inward(own):
    total = own
    for step in fold_steps()[:-1]:
        came = lax.ppermute(total, "tensor", line_pairs(step))
        total = (total.astype(F32) + came.astype(F32)).astype(BF16)
    return total


def outward(block, depth):
    for step in reversed(fold_steps()[:-1]):
        came = lax.ppermute(block, "tensor", [(b, a) for a, b in line_pairs(step)])
        block = jnp.where(depth[:, : block.shape[-1]] == step, came, block)
    return block


def swap(into, out, depth):
    if not fold_steps():
        return jnp.zeros_like(into if out is None else out)
    inner = len(fold_steps()) - 1
    pairs = line_pairs(inner)
    back = [(b, a) for a, b in pairs]
    if out is None:
        return lax.ppermute(into, "tensor", pairs)
    if into is None:
        return lax.ppermute(out, "tensor", back)
    block = jnp.where(depth[:, : out.shape[-1]] > inner, out, into)
    return lax.ppermute(block, "tensor", pairs + back)


def across(block):
    half = lax.axis_size("tensor") // 2
    return lax.ppermute(block, "tensor", [(half - 1, half), (half, half - 1)])


def activations(gate, up, grad_hidden):
    sigma = jax.nn.sigmoid(gate)
    silu = gate * sigma
    return jnp.stack(
        [
            silu * up,
            grad_hidden * up * sigma * (1.0 + gate * (1.0 - sigma)),
            grad_hidden * silu,
        ]
    ).astype(BF16)


def shards(tokens, gate_weight, up_weight, down_weight, out_grad):
    mine, width = tokens.shape
    peers = lax.axis_size("dp")
    step = STEP if mine % STEP == 0 else mine
    chunks = mine // step
    half = peers * step // 2
    far, depth, signs, bits, depths = my_row(max(width, gate_weight.shape[1]))
    far = far[:, :width] > 0.5

    both = jnp.stack([tokens, out_grad])

    def arrive(turned):
        low, high = gather_dp(turned.reshape(2, -1, 1, step, width), 2)
        other, own = jnp.where(far, low, high), jnp.where(far, high, low)
        return [part.reshape(2, -1, half, width) for part in (other, own)]

    first = min(2, chunks)
    early = spread(both[:, : first * step])
    late = spread(after(both[:, first * step :], early[1])) if chunks > first else None
    groups = [arrive(rotate(early, signs).astype(BF16))]

    def leave(blocks):
        sums = []
        for block in blocks:
            mixed = dot(block[0], down_weight, 1, 0)
            grads = dot(block[1], gate_weight, 1, 1) + dot(block[2], up_weight, 1, 1)
            sums.append(jnp.stack([mixed, grads]))
        sums = jnp.concatenate(sums, axis=1).reshape(2, -1, 2, half, width)
        low = jnp.where(far, sums[:, :, 0], sums[:, :, 1])
        return low, jnp.where(far, sums[:, :, 1], sums[:, :, 0]).astype(BF16)

    def done(i):
        parts = []
        for k in (2 * i + 1, 2 * i):
            inner = depth[:, : outs[k].shape[-1]] > len(fold_steps()) - 1
            parts.append(outward(jnp.where(inner, outs[k], came[k + LAG]), depth))
        return jnp.concatenate(parts, axis=1)

    steps = 2 * chunks
    split, ends = max(chunks - 2, 0), []
    messages, came, crossed, acts, outs = [], [], [], [], []
    for s in range(steps + LAG):
        if s < steps:
            i, which = divmod(s, 2)
            group, place = (groups[0], i) if i < first else (groups[1], i - first)
            x, g = group[which][0, place], group[which][1, place]
            if s > 0:
                other = came[s - 2] if s > 1 else messages[0][2:]
                x, g = after(x, other), after(g, other)
            parts = [dot(x, gate_weight, 1, 0), dot(x, up_weight, 1, 0), dot(g, down_weight, 1, 1)]
            message = jnp.stack(parts).astype(BF16)
            messages.append(inward(after(message, came[0]) if s == 1 else message))
        if s == steps + LAG - 1 and split > 0:
            low, high = leave([done(i) for i in range(split)])
            sums, _, last = scatter_dp(low, high)
            ends.append(rotate_by_halves(sums.reshape(2, -1, width), bits))
            outs[-1] = after(outs[-1], last)
        came.append(
            swap(
                messages[s] if s < steps else None,
                outs[s - LAG] if s >= LAG else None,
                depths[s % 2],
            )
        )
        if s == 0 and chunks > first:
            tick = exchange(message[2, :step, :width], "dp", 1)
            late[0] = after(late[0], tick)
            groups.append(arrive(rotate(late, signs).astype(BF16)))
        if s < steps:
            total = messages[s].astype(F32) + came[s].astype(F32)
            if which == 0:
                other_sums = across(total.astype(BF16))
            else:
                gate, up, grad_hidden = total + other_sums.astype(F32)
                acts.append(activations(gate, up, grad_hidden))
                crossed.append(across(acts[i]))
                outs += [acts[i], crossed[i]]
    low, high = leave([done(i) for i in range(split, chunks)])
    sums, _, _ = scatter_dp(low, high)
    ends.append(rotate(spread(sums.reshape(2, -1, width).astype(BF16)), signs))
    ends = jnp.concatenate(ends, axis=1)

    acts = jnp.concatenate([done(i) for i in range(chunks)], axis=1)
    rows = [jnp.stack(group, axis=2).reshape(2, -1, width) for group in groups]
    rows = after(jnp.concatenate(rows, axis=1), high[0, 0, :1])
    factor = 1.0 / math.sqrt(rows.shape[1])
    return (
        ends[0],
        ends[1],
        (dot(rows[0], acts[1], 0, 0) * factor).astype(BF16),
        (dot(rows[0], acts[2], 0, 0) * factor).astype(BF16),
        (dot(acts[0], rows[1], 0, 0) * factor).astype(BF16),
    )


def solution(mesh):
    return jax.shard_map(
        shards,
        mesh=mesh,
        in_specs=(
            P("dp", "tensor"),
            P("tensor", "dp"),
            P("tensor", "dp"),
            P("dp", "tensor"),
            P("dp", "tensor"),
        ),
        out_specs=(
            P("dp", "tensor"),
            P("dp", "tensor"),
            P("tensor", "dp"),
            P("tensor", "dp"),
            P("dp", "tensor"),
        ),
        check_vma=False,
    )
```

```python
import math

import jax
import jax.numpy as jnp
import numpy as np
from jax import lax
from jax.sharding import PartitionSpec as P

D = 2048
BF16 = jnp.bfloat16
F32 = jnp.float32
STEP = 16
LAG = 3
KINDS = 4


def sylvester(order):
    table = np.ones((1, 1), np.float32)
    while table.shape[0] < order:
        table = np.block([[table, table], [table, -table]])
    return table


def dot(left, right, left_dim, right_dim):
    return lax.dot_general(
        left, right, (((left_dim,), (right_dim,)), ((), ())), preferred_element_type=F32
    )


def after(block, other):
    other = other.reshape((-1,) + other.shape[-2:])[0]
    if other.shape[0] < block.shape[-2]:
        other = other[:1]
    other = other[: block.shape[-2]]
    wide = block.shape[-1]
    if other.shape[-1] < wide:
        other = jnp.concatenate([other] * (-(-wide // other.shape[-1])), axis=-1)
    other = other[:, :wide].astype(block.dtype)
    return jnp.where(jnp.isnan(other), other, block)


def my_row(length):
    groups = lax.axis_size("tensor")
    signs = sylvester(groups)
    me = np.arange(groups)
    away = np.minimum(me, groups - 1 - me)
    columns = [me >= groups // 2, away]
    columns += [signs[me, me ^ apart] for apart in range(groups)]
    columns += [1 - 2 * (me >> bit & 1) for bit in range(groups.bit_length() - 1)]
    columns += [away] * KINDS
    table = np.stack(columns, axis=1).astype(np.float32)[:, :, None, None]
    table = jnp.asarray(np.tile(table, (1, 1, 1, length)))
    row = lax.dynamic_index_in_dim(table, lax.axis_index("tensor"), keepdims=False)
    return row[0], row[1], row[2 : 2 + groups], row[2 + groups : -KINDS], row[-KINDS:]


def exchange(block, axis, apart):
    count = lax.axis_size(axis)
    return lax.ppermute(block, axis, [(i, i ^ apart) for i in range(count)])


def spread(block):
    return [block] + [exchange(block, "tensor", k) for k in range(1, lax.axis_size("tensor"))]


def turn(block):
    width = block.shape[-1]
    square = jnp.asarray(sylvester(width), BF16)
    rows = block.reshape(-1, width) * (1.0 / math.sqrt(D))
    high = lax.reduce_precision(rows, 8, 7)
    low = (rows - high).astype(BF16)
    return (dot(high.astype(BF16), square, 1, 0) + dot(low, square, 1, 0)).reshape(block.shape)


def rotate(pieces, signs):
    width = pieces[0].shape[-1]
    return turn(sum(piece.astype(F32) * sign[:, :width] for piece, sign in zip(pieces, signs)))


def rotate_by_halves(block, bits):
    block = turn(block)
    for level, bit in enumerate(bits):
        came = exchange(block.astype(BF16), "tensor", 1 << level)
        block = block * bit[:, : block.shape[-1]] + came.astype(F32)
    return block


def dp_stages():
    bits = [1 << bit for bit in reversed(range(lax.axis_size("dp").bit_length() - 1))]
    stages = []
    while len(bits) > 1:
        high, low, bits = bits[0], bits[1], bits[2:]
        stages.append([0, low, high, high | low])
    if bits:
        stages.append([0, bits[0]])
    return stages


def gather_dp(block, axis, ahead):
    stages = dp_stages()
    for stage in stages[:-1]:
        came = [exchange(block, "dp", apart) for apart in stage[1:]]
        for other in ahead:
            block = after(block, other)
        block = jnp.concatenate([block] + came, axis=axis)
    return block, exchange(block, "dp", stages[-1][1])


def scatter_dp(low, high):
    stages = dp_stages()
    first = exchange(high, "dp", stages[-1][1])
    low, came = low + first.astype(F32), first
    for stage in reversed(stages[:-1]):
        low = low.reshape(low.shape[:2] + (len(stage), -1) + low.shape[-1:])
        total = low[:, :, 0]
        for place, apart in enumerate(stage[1:], 1):
            came = exchange(low[:, :, place].astype(BF16), "dp", apart)
            total = total + came.astype(F32)
        low = total
    return low, first, came


def line_pairs(step):
    last = lax.axis_size("tensor") - 1
    return [(step, step + 1), (last - step, last - step - 1)]


def fold_steps():
    return range(lax.axis_size("tensor") // 2 - 1)


def inward(own):
    total = own
    for step in fold_steps()[:-1]:
        came = lax.ppermute(total, "tensor", line_pairs(step))
        total = (total.astype(F32) + came.astype(F32)).astype(BF16)
    return total


def outward(block, depth):
    for step in reversed(fold_steps()[:-1]):
        came = lax.ppermute(block, "tensor", [(b, a) for a, b in line_pairs(step)])
        block = jnp.where(depth[:, : block.shape[-1]] == step, came, block)
    return block


def swap(into, out, depth):
    if not fold_steps():
        return jnp.zeros_like(into if out is None else out)
    inner = len(fold_steps()) - 1
    pairs = line_pairs(inner)
    back = [(b, a) for a, b in pairs]
    if out is None:
        return lax.ppermute(into, "tensor", pairs)
    if into is None:
        return lax.ppermute(out, "tensor", back)
    block = jnp.where(depth[:, : out.shape[-1]] > inner, out, into)
    return lax.ppermute(block, "tensor", pairs + back)


def across(block):
    half = lax.axis_size("tensor") // 2
    return lax.ppermute(block, "tensor", [(half - 1, half), (half, half - 1)])


def activations(gate, up, grad_hidden):
    sigma = jax.nn.sigmoid(gate)
    silu = gate * sigma
    return jnp.stack(
        [
            silu * up,
            grad_hidden * up * sigma * (1.0 + gate * (1.0 - sigma)),
            grad_hidden * silu,
        ]
    ).astype(BF16)


def shards(tokens, gate_weight, up_weight, down_weight, out_grad):
    mine, width = tokens.shape
    peers = lax.axis_size("dp")
    step = STEP if mine % STEP == 0 else mine
    chunks = mine // step
    half = peers * step // 2
    far, depth, signs, bits, depths = my_row(max(width, gate_weight.shape[1]))
    far = far[:, :width] > 0.5

    both = jnp.stack([tokens, out_grad])

    def arrive(turned, ahead=()):
        low, high = gather_dp(turned.reshape(2, -1, 1, step, width), 2, ahead)
        other, own = jnp.where(far, low, high), jnp.where(far, high, low)
        return [part.reshape(2, -1, half, width) for part in (other, own)]

    first = min(2, chunks)
    early = spread(both[:, : first * step])
    late = spread(after(both[:, first * step :], early[1])) if chunks > first else None
    groups = [arrive(rotate(early, signs).astype(BF16))]

    def leave(blocks):
        sums = []
        for block in blocks:
            mixed = dot(block[0], down_weight, 1, 0)
            grads = dot(block[1], gate_weight, 1, 1) + dot(block[2], up_weight, 1, 1)
            sums.append(jnp.stack([mixed, grads]))
        sums = jnp.concatenate(sums, axis=1).reshape(2, -1, 2, half, width)
        low = jnp.where(far, sums[:, :, 0], sums[:, :, 1])
        return low, jnp.where(far, sums[:, :, 1], sums[:, :, 0]).astype(BF16)

    def done(i):
        parts = []
        for k in (2 * i + 1, 2 * i):
            inner = depth[:, : outs[k].shape[-1]] > len(fold_steps()) - 1
            parts.append(outward(jnp.where(inner, outs[k], came[k + LAG]), depth))
        return jnp.concatenate(parts, axis=1)

    steps = 2 * chunks
    split, ends = max(chunks - 2, 0), []
    messages, came, crossed, acts, outs = [], [], [], [], []
    for s in range(steps + LAG):
        if s < steps:
            i, which = divmod(s, 2)
            group, place = (groups[0], i) if i < first else (groups[1], i - first)
            x, g = group[which][0, place], group[which][1, place]
            if s > 0:
                other = came[max(s - LAG, 0)] if s > 1 else messages[0][2:]
                x, g = after(x, other), after(g, other)
            parts = [dot(x, gate_weight, 1, 0), dot(x, up_weight, 1, 0), dot(g, down_weight, 1, 1)]
            message = jnp.stack(parts).astype(BF16)
            messages.append(inward(after(message, came[0]) if s == 1 else message))
        if s == steps + LAG - 1 and split > 0:
            low, high = leave([done(i) for i in range(split)])
            sums, early, ahead = scatter_dp(low, high)
            ends.append(rotate_by_halves(sums.reshape(2, -1, width), bits))
            outs[-1] = after(outs[-1], early)
        came.append(
            swap(
                messages[s] if s < steps else None,
                outs[s - LAG] if s >= LAG else None,
                depths[s % KINDS],
            )
        )
        if s == 0 and chunks > first:
            tick = exchange(message[2, :step, :width], "dp", 1)
            late[0] = after(late[0], tick)
        if s == 1 and chunks > first:
            groups.append(arrive(rotate(late, signs).astype(BF16), [messages[1], middle]))
        if s < steps:
            total = messages[s].astype(F32) + came[s].astype(F32)
            if which == 0:
                middle = total.astype(BF16)
                other_sums = across(middle)
            else:
                gate, up, grad_hidden = total + other_sums.astype(F32)
                acts.append(activations(gate, up, grad_hidden))
                crossed.append(across(acts[i]))
                outs += [acts[i], crossed[i]]
    low, high = leave([done(i) for i in range(split, chunks)])
    high = after(high, ahead) if split > 0 else high
    sums, _, _ = scatter_dp(low, high)
    ends.append(rotate(spread(sums.reshape(2, -1, width).astype(BF16)), signs))
    ends = jnp.concatenate(ends, axis=1)

    acts = jnp.concatenate([done(i) for i in range(chunks)], axis=1)
    rows = [jnp.stack(group, axis=2).reshape(2, -1, width) for group in groups]
    rows = after(jnp.concatenate(rows, axis=1), high[0, 0, :1])
    factor = 1.0 / math.sqrt(rows.shape[1])
    return (
        ends[0],
        ends[1],
        (dot(rows[0], acts[1], 0, 0) * factor).astype(BF16),
        (dot(rows[0], acts[2], 0, 0) * factor).astype(BF16),
        (dot(acts[0], rows[1], 0, 0) * factor).astype(BF16),
    )


def solution(mesh):
    return jax.shard_map(
        shards,
        mesh=mesh,
        in_specs=(
            P("dp", "tensor"),
            P("tensor", "dp"),
            P("tensor", "dp"),
            P("dp", "tensor"),
            P("dp", "tensor"),
        ),
        out_specs=(
            P("dp", "tensor"),
            P("dp", "tensor"),
            P("tensor", "dp"),
            P("tensor", "dp"),
            P("dp", "tensor"),
        ),
        check_vma=False,
    )
```

```python
import math

import jax
import jax.numpy as jnp
import numpy as np
from jax import lax
from jax.sharding import PartitionSpec as P

D = 2048
BF16 = jnp.bfloat16
F32 = jnp.float32
STEP = 16
LAG = 3
KINDS = 4


def sylvester(order):
    table = np.ones((1, 1), np.float32)
    while table.shape[0] < order:
        table = np.block([[table, table], [table, -table]])
    return table


def dot(left, right, left_dim, right_dim):
    return lax.dot_general(
        left, right, (((left_dim,), (right_dim,)), ((), ())), preferred_element_type=F32
    )


def after(block, other):
    other = other.reshape((-1,) + other.shape[-2:])[0]
    if other.shape[0] < block.shape[-2]:
        other = other[:1]
    other = other[: block.shape[-2]]
    wide = block.shape[-1]
    if other.shape[-1] < wide:
        other = jnp.concatenate([other] * (-(-wide // other.shape[-1])), axis=-1)
    other = other[:, :wide].astype(block.dtype)
    return jnp.where(jnp.isnan(other), other, block)


def my_row(length):
    groups = lax.axis_size("tensor")
    signs = sylvester(groups)
    me = np.arange(groups)
    away = np.minimum(me, groups - 1 - me)
    columns = [me >= groups // 2, away]
    columns += [signs[me, me ^ apart] for apart in range(groups)]
    columns += [1 - 2 * (me >> bit & 1) for bit in range(groups.bit_length() - 1)]
    columns += [away] * KINDS
    table = np.stack(columns, axis=1).astype(np.float32)[:, :, None, None]
    table = jnp.asarray(np.tile(table, (1, 1, 1, length)))
    row = lax.dynamic_index_in_dim(table, lax.axis_index("tensor"), keepdims=False)
    return row[0], row[1], row[2 : 2 + groups], row[2 + groups : -KINDS], row[-KINDS:]


def exchange(block, axis, apart):
    count = lax.axis_size(axis)
    return lax.ppermute(block, axis, [(i, i ^ apart) for i in range(count)])


def spread(block):
    return [block] + [exchange(block, "tensor", k) for k in range(1, lax.axis_size("tensor"))]


def turn(block):
    width = block.shape[-1]
    square = jnp.asarray(sylvester(width), BF16)
    rows = block.reshape(-1, width) * (1.0 / math.sqrt(D))
    high = lax.reduce_precision(rows, 8, 7)
    low = (rows - high).astype(BF16)
    return (dot(high.astype(BF16), square, 1, 0) + dot(low, square, 1, 0)).reshape(block.shape)


def rotate(pieces, signs):
    width = pieces[0].shape[-1]
    return turn(sum(piece.astype(F32) * sign[:, :width] for piece, sign in zip(pieces, signs)))


def rotate_by_halves(block, bits):
    block = turn(block)
    for level, bit in enumerate(bits):
        came = exchange(block.astype(BF16), "tensor", 1 << level)
        block = block * bit[:, : block.shape[-1]] + came.astype(F32)
    return block


def dp_stages():
    bits = [1 << bit for bit in reversed(range(lax.axis_size("dp").bit_length() - 1))]
    stages = []
    while len(bits) > 1:
        high, low, bits = bits[0], bits[1], bits[2:]
        stages.append([0, low, high, high | low])
    if bits:
        stages.append([0, bits[0]])
    return stages


def gather_dp(block, axis, ahead):
    stages = dp_stages()
    for stage in stages[:-1]:
        came = [exchange(block, "dp", apart) for apart in stage[1:]]
        for other in ahead:
            block = after(block, other)
        block = jnp.concatenate([block] + came, axis=axis)
    return block, exchange(block, "dp", stages[-1][1])


def scatter_dp(low, high):
    stages = dp_stages()
    first = exchange(high, "dp", stages[-1][1])
    low, came = low + first.astype(F32), first
    for stage in reversed(stages[:-1]):
        low = low.reshape(low.shape[:2] + (len(stage), -1) + low.shape[-1:])
        total = low[:, :, 0]
        for place, apart in enumerate(stage[1:], 1):
            came = exchange(low[:, :, place].astype(BF16), "dp", apart)
            total = total + came.astype(F32)
        low = total
    return low, first, came


def line_pairs(step):
    last = lax.axis_size("tensor") - 1
    return [(step, step + 1), (last - step, last - step - 1)]


def fold_steps():
    return range(lax.axis_size("tensor") // 2 - 1)


def inward(own):
    total = own
    for step in fold_steps()[:-1]:
        came = lax.ppermute(total, "tensor", line_pairs(step))
        total = (total.astype(F32) + came.astype(F32)).astype(BF16)
    return total


def outward(block, depth):
    for step in reversed(fold_steps()[:-1]):
        came = lax.ppermute(block, "tensor", [(b, a) for a, b in line_pairs(step)])
        block = jnp.where(depth[:, : block.shape[-1]] == step, came, block)
    return block


def swap(into, out, depth):
    if not fold_steps():
        return jnp.zeros_like(into if out is None else out)
    inner = len(fold_steps()) - 1
    pairs = line_pairs(inner)
    back = [(b, a) for a, b in pairs]
    if out is None:
        return lax.ppermute(into, "tensor", pairs)
    if into is None:
        return lax.ppermute(out, "tensor", back)
    block = jnp.where(depth[:, : out.shape[-1]] > inner, out, into)
    return lax.ppermute(block, "tensor", pairs + back)


def across(block):
    half = lax.axis_size("tensor") // 2
    return lax.ppermute(block, "tensor", [(half - 1, half), (half, half - 1)])


def activations(gate, up, grad_hidden):
    sigma = jax.nn.sigmoid(gate)
    silu = gate * sigma
    return jnp.stack(
        [
            silu * up,
            grad_hidden * up * sigma * (1.0 + gate * (1.0 - sigma)),
            grad_hidden * silu,
        ]
    ).astype(BF16)


def shards(tokens, gate_weight, up_weight, down_weight, out_grad):
    mine, width = tokens.shape
    peers = lax.axis_size("dp")
    step = STEP if mine % STEP == 0 else mine
    chunks = mine // step
    half = peers * step // 2
    far, depth, signs, bits, depths = my_row(max(width, gate_weight.shape[1]))
    far = far[:, :width] > 0.5

    both = jnp.stack([tokens, out_grad])

    def arrive(turned, ahead=()):
        low, high = gather_dp(turned.reshape(2, -1, 1, step, width), 2, ahead)
        other, own = jnp.where(far, low, high), jnp.where(far, high, low)
        return [part.reshape(2, -1, half, width) for part in (other, own)]

    first = min(2, chunks)
    early = spread(both[:, : first * step])
    late = spread(after(both[:, first * step :], early[1])) if chunks > first else None
    groups = [arrive(rotate(early, signs).astype(BF16))]

    def leave(blocks):
        sums = []
        for block in blocks:
            mixed = dot(block[0], down_weight, 1, 0)
            grads = dot(block[1], gate_weight, 1, 1) + dot(block[2], up_weight, 1, 1)
            sums.append(jnp.stack([mixed, grads]))
        sums = jnp.concatenate(sums, axis=1).reshape(2, -1, 2, half, width)
        low = jnp.where(far, sums[:, :, 0], sums[:, :, 1])
        return low, jnp.where(far, sums[:, :, 1], sums[:, :, 0]).astype(BF16)

    def done(i):
        parts = []
        for k in (2 * i + 1, 2 * i):
            inner = depth[:, : outs[k].shape[-1]] > len(fold_steps()) - 1
            parts.append(outward(jnp.where(inner, outs[k], came[k + LAG]), depth))
        return jnp.concatenate(parts, axis=1)

    steps = 2 * chunks
    split, ends = max(chunks - 2, 0), []
    messages, came, crossed, acts, outs = [], [], [], [], []
    for s in range(steps + LAG):
        if s < steps:
            i, which = divmod(s, 2)
            group, place = (groups[0], i) if i < first else (groups[1], i - first)
            x, g = group[which][0, place], group[which][1, place]
            if s > 0:
                other = acts[i - 2] if i > 1 else middle if i == 1 else messages[0][2:]
                x, g = after(x, other), after(g, other)
            parts = [dot(x, gate_weight, 1, 0), dot(x, up_weight, 1, 0), dot(g, down_weight, 1, 1)]
            message = jnp.stack(parts).astype(BF16)
            messages.append(inward(after(message, came[0]) if s == 1 else message))
        if s == steps + LAG - 1 and split > 0:
            low, high = leave([done(i) for i in range(split)])
            first_sums, ahead, _ = scatter_dp(low, high)
            outs[-1] = after(outs[-1], ahead)
        came.append(
            swap(
                messages[s] if s < steps else None,
                outs[s - LAG] if s >= LAG else None,
                depths[s % KINDS],
            )
        )
        if s == 0 and chunks > first:
            tick = exchange(message[2, :step, :width], "dp", 1)
            late[0] = after(late[0], tick)
        if s == 1 and chunks > first:
            groups.append(arrive(rotate(late, signs).astype(BF16), [messages[1], middle]))
        if s < steps:
            total = messages[s].astype(F32) + came[s].astype(F32)
            if which == 0:
                middle = total.astype(BF16)
                other_sums = across(middle)
            else:
                gate, up, grad_hidden = total + other_sums.astype(F32)
                acts.append(activations(gate, up, grad_hidden))
                crossed.append(across(acts[i]))
                outs += [acts[i], crossed[i]]
    low, high = leave([done(i) for i in range(split, chunks)])
    if split > 0:
        first_sums = after(first_sums.reshape(2, -1, width), came[-1])
        ends.append(rotate_by_halves(first_sums, bits))
    sums, _, _ = scatter_dp(low, high)
    ends.append(rotate(spread(sums.reshape(2, -1, width).astype(BF16)), signs))
    ends = jnp.concatenate(ends, axis=1)

    acts = jnp.concatenate([done(i) for i in range(chunks)], axis=1)
    rows = [jnp.stack(group, axis=2).reshape(2, -1, width) for group in groups]
    rows = after(jnp.concatenate(rows, axis=1), high[0, 0, :1])
    factor = 1.0 / math.sqrt(rows.shape[1])
    return (
        ends[0],
        ends[1],
        (dot(rows[0], acts[1], 0, 0) * factor).astype(BF16),
        (dot(rows[0], acts[2], 0, 0) * factor).astype(BF16),
        (dot(acts[0], rows[1], 0, 0) * factor).astype(BF16),
    )


def solution(mesh):
    return jax.shard_map(
        shards,
        mesh=mesh,
        in_specs=(
            P("dp", "tensor"),
            P("tensor", "dp"),
            P("tensor", "dp"),
            P("dp", "tensor"),
            P("dp", "tensor"),
        ),
        out_specs=(
            P("dp", "tensor"),
            P("dp", "tensor"),
            P("tensor", "dp"),
            P("tensor", "dp"),
            P("dp", "tensor"),
        ),
        check_vma=False,
    )
```

```python
import math

import jax
import jax.numpy as jnp
import numpy as np
from jax import lax
from jax.sharding import PartitionSpec as P

D = 2048
BF16 = jnp.bfloat16
F32 = jnp.float32
STEP = 16
LAG = 3
KINDS = 4


def sylvester(order):
    table = np.ones((1, 1), np.float32)
    while table.shape[0] < order:
        table = np.block([[table, table], [table, -table]])
    return table


def dot(left, right, left_dim, right_dim):
    return lax.dot_general(
        left, right, (((left_dim,), (right_dim,)), ((), ())), preferred_element_type=F32
    )


def after(block, other):
    other = other.reshape((-1,) + other.shape[-2:])[0]
    if other.shape[0] < block.shape[-2]:
        other = other[:1]
    other = other[: block.shape[-2]]
    wide = block.shape[-1]
    if other.shape[-1] < wide:
        other = jnp.concatenate([other] * (-(-wide // other.shape[-1])), axis=-1)
    other = other[:, :wide].astype(block.dtype)
    return jnp.where(jnp.isnan(other), other, block)


def my_row(length):
    groups = lax.axis_size("tensor")
    signs = sylvester(groups)
    me = np.arange(groups)
    away = np.minimum(me, groups - 1 - me)
    columns = [me >= groups // 2, away]
    columns += [signs[me, me ^ apart] for apart in range(groups)]
    columns += [1 - 2 * (me >> bit & 1) for bit in range(groups.bit_length() - 1)]
    columns += [away] * KINDS
    table = np.stack(columns, axis=1).astype(np.float32)[:, :, None, None]
    table = jnp.asarray(np.tile(table, (1, 1, 1, length)))
    row = lax.dynamic_index_in_dim(table, lax.axis_index("tensor"), keepdims=False)
    return row[0], row[1], row[2 : 2 + groups], row[2 + groups : -KINDS], row[-KINDS:]


def exchange(block, axis, apart):
    count = lax.axis_size(axis)
    return lax.ppermute(block, axis, [(i, i ^ apart) for i in range(count)])


def spread(block):
    return [block] + [exchange(block, "tensor", k) for k in range(1, lax.axis_size("tensor"))]


def turn(block):
    width = block.shape[-1]
    square = jnp.asarray(sylvester(width), BF16)
    rows = block.reshape(-1, width) * (1.0 / math.sqrt(D))
    high = lax.reduce_precision(rows, 8, 7)
    low = (rows - high).astype(BF16)
    return (dot(high.astype(BF16), square, 1, 0) + dot(low, square, 1, 0)).reshape(block.shape)


def rotate(pieces, signs):
    width = pieces[0].shape[-1]
    return turn(sum(piece.astype(F32) * sign[:, :width] for piece, sign in zip(pieces, signs)))


def rotate_by_halves(block, bits):
    block = turn(block)
    for level, bit in enumerate(bits):
        came = exchange(block.astype(BF16), "tensor", 1 << level)
        block = block * bit[:, : block.shape[-1]] + came.astype(F32)
    return block


def dp_stages():
    bits = [1 << bit for bit in reversed(range(lax.axis_size("dp").bit_length() - 1))]
    stages = []
    while len(bits) > 1:
        high, low, bits = bits[0], bits[1], bits[2:]
        stages.append([0, low, high, high | low])
    if bits:
        stages.append([0, bits[0]])
    return stages


def gather_dp(block, axis, ahead):
    stages = dp_stages()
    for stage in stages[:-1]:
        came = [exchange(block, "dp", apart) for apart in stage[1:]]
        for other in ahead:
            block = after(block, other)
        block = jnp.concatenate([block] + came, axis=axis)
    return block, exchange(block, "dp", stages[-1][1])


def scatter_dp(low, high):
    stages = dp_stages()
    first = exchange(high, "dp", stages[-1][1])
    low, came = low + first.astype(F32), first
    for stage in reversed(stages[:-1]):
        low = low.reshape(low.shape[:2] + (len(stage), -1) + low.shape[-1:])
        total = low[:, :, 0]
        for place, apart in enumerate(stage[1:], 1):
            came = exchange(low[:, :, place].astype(BF16), "dp", apart)
            total = total + came.astype(F32)
        low = total
    return low, first, came


def line_pairs(step):
    last = lax.axis_size("tensor") - 1
    return [(step, step + 1), (last - step, last - step - 1)]


def fold_steps():
    return range(lax.axis_size("tensor") // 2 - 1)


def inward(own):
    total = own
    for step in fold_steps()[:-1]:
        came = lax.ppermute(total, "tensor", line_pairs(step))
        total = (total.astype(F32) + came.astype(F32)).astype(BF16)
    return total


def outward(block, depth):
    for step in reversed(fold_steps()[:-1]):
        came = lax.ppermute(block, "tensor", [(b, a) for a, b in line_pairs(step)])
        block = jnp.where(depth[:, : block.shape[-1]] == step, came, block)
    return block


def swap(into, out, depth):
    if not fold_steps():
        return jnp.zeros_like(into if out is None else out)
    inner = len(fold_steps()) - 1
    pairs = line_pairs(inner)
    back = [(b, a) for a, b in pairs]
    if out is None:
        return lax.ppermute(into, "tensor", pairs)
    if into is None:
        return lax.ppermute(out, "tensor", back)
    block = jnp.where(depth[:, : out.shape[-1]] > inner, out, into)
    return lax.ppermute(block, "tensor", pairs + back)


def across(block):
    half = lax.axis_size("tensor") // 2
    return lax.ppermute(block, "tensor", [(half - 1, half), (half, half - 1)])


def activations(gate, up, grad_hidden):
    sigma = jax.nn.sigmoid(gate)
    silu = gate * sigma
    return jnp.stack(
        [
            silu * up,
            grad_hidden * up * sigma * (1.0 + gate * (1.0 - sigma)),
            grad_hidden * silu,
        ]
    ).astype(BF16)


def shards(tokens, gate_weight, up_weight, down_weight, out_grad):
    mine, width = tokens.shape
    peers = lax.axis_size("dp")
    step = STEP if mine % STEP == 0 else mine
    chunks = mine // step
    half = peers * step // 2
    far, depth, signs, bits, depths = my_row(max(width, gate_weight.shape[1]))
    far = far[:, :width] > 0.5

    both = jnp.stack([tokens, out_grad])

    def arrive(turned, ahead=()):
        low, high = gather_dp(turned.reshape(2, -1, 1, step, width), 2, ahead)
        other, own = jnp.where(far, low, high), jnp.where(far, high, low)
        return [part.reshape(2, -1, half, width) for part in (other, own)]

    first = min(2, chunks)
    early = spread(both[:, : first * step])
    late = spread(after(both[:, first * step :], early[1])) if chunks > first else None
    groups = [arrive(rotate(early, signs).astype(BF16))]

    def leave(blocks):
        sums = []
        for block in blocks:
            mixed = dot(block[0], down_weight, 1, 0)
            grads = dot(block[1], gate_weight, 1, 1) + dot(block[2], up_weight, 1, 1)
            sums.append(jnp.stack([mixed, grads]))
        sums = jnp.concatenate(sums, axis=1).reshape(2, -1, 2, half, width)
        low = jnp.where(far, sums[:, :, 0], sums[:, :, 1])
        return low, jnp.where(far, sums[:, :, 1], sums[:, :, 0]).astype(BF16)

    def done(i):
        parts = []
        for k in (2 * i + 1, 2 * i):
            inner = depth[:, : outs[k].shape[-1]] > len(fold_steps()) - 1
            parts.append(outward(jnp.where(inner, outs[k], came[k + LAG]), depth))
        return jnp.concatenate(parts, axis=1)

    steps = 2 * chunks
    split, ends = max(chunks - 2, 0), []
    messages, came, crossed, acts, outs = [], [], [], [], []
    for s in range(steps + LAG):
        if s < steps:
            i, which = divmod(s, 2)
            group, place = (groups[0], i) if i < first else (groups[1], i - first)
            x, g = group[which][0, place], group[which][1, place]
            if s > 0:
                other = acts[i - 2] if i > 3 else came[max(s - LAG, 0)] if s > 1 else messages[0][2:]
                x, g = after(x, other), after(g, other)
            parts = [dot(x, gate_weight, 1, 0), dot(x, up_weight, 1, 0), dot(g, down_weight, 1, 1)]
            message = jnp.stack(parts).astype(BF16)
            messages.append(inward(after(message, came[0]) if s == 1 else message))
        if s == steps + LAG - 1 and split > 0:
            low, high = leave([done(i) for i in range(split)])
            first_sums, ahead, _ = scatter_dp(low, high)
            outs[-1] = after(outs[-1], ahead)
        came.append(
            swap(
                messages[s] if s < steps else None,
                outs[s - LAG] if s >= LAG else None,
                depths[s % KINDS],
            )
        )
        if s == 0 and chunks > first:
            tick = exchange(message[2, :step, :width], "dp", 1)
            late[0] = after(late[0], tick)
        if s == 1 and chunks > first:
            groups.append(arrive(rotate(late, signs).astype(BF16), [messages[1], middle]))
        if s < steps:
            total = messages[s].astype(F32) + came[s].astype(F32)
            if which == 0:
                middle = total.astype(BF16)
                other_sums = across(middle)
            else:
                gate, up, grad_hidden = total + other_sums.astype(F32)
                acts.append(activations(gate, up, grad_hidden))
                crossed.append(across(acts[i]))
                outs += [acts[i], crossed[i]]
    low, high = leave([done(i) for i in range(split, chunks)])
    if split > 0:
        first_sums = after(first_sums.reshape(2, -1, width), came[-1])
        ends.append(rotate_by_halves(first_sums, bits))
    sums, _, _ = scatter_dp(low, high)
    ends.append(rotate(spread(sums.reshape(2, -1, width).astype(BF16)), signs))
    ends = jnp.concatenate(ends, axis=1)

    acts = jnp.concatenate([done(i) for i in range(chunks)], axis=1)
    rows = [jnp.stack(group, axis=2).reshape(2, -1, width) for group in groups]
    rows = after(jnp.concatenate(rows, axis=1), high[0, 0, :1])
    factor = 1.0 / math.sqrt(rows.shape[1])
    return (
        ends[0],
        ends[1],
        (dot(rows[0], acts[1], 0, 0) * factor).astype(BF16),
        (dot(rows[0], acts[2], 0, 0) * factor).astype(BF16),
        (dot(acts[0], rows[1], 0, 0) * factor).astype(BF16),
    )


def solution(mesh):
    return jax.shard_map(
        shards,
        mesh=mesh,
        in_specs=(
            P("dp", "tensor"),
            P("tensor", "dp"),
            P("tensor", "dp"),
            P("dp", "tensor"),
            P("dp", "tensor"),
        ),
        out_specs=(
            P("dp", "tensor"),
            P("dp", "tensor"),
            P("tensor", "dp"),
            P("tensor", "dp"),
            P("dp", "tensor"),
        ),
        check_vma=False,
    )
```

```python
import math

import jax
import jax.numpy as jnp
import numpy as np
from jax import lax
from jax.sharding import PartitionSpec as P

D = 2048
BF16 = jnp.bfloat16
F32 = jnp.float32
STEP = 16
LAG = 3
KINDS = 4


def sylvester(order):
    table = np.ones((1, 1), np.float32)
    while table.shape[0] < order:
        table = np.block([[table, table], [table, -table]])
    return table


def dot(left, right, left_dim, right_dim):
    return lax.dot_general(
        left, right, (((left_dim,), (right_dim,)), ((), ())), preferred_element_type=F32
    )


def after(block, other):
    other = other.reshape((-1,) + other.shape[-2:])[0]
    if other.shape[0] < block.shape[-2]:
        other = other[:1]
    other = other[: block.shape[-2]]
    wide = block.shape[-1]
    if other.shape[-1] < wide:
        other = jnp.concatenate([other] * (-(-wide // other.shape[-1])), axis=-1)
    other = other[:, :wide].astype(block.dtype)
    return jnp.where(jnp.isnan(other), other, block)


def my_row(length):
    groups = lax.axis_size("tensor")
    signs = sylvester(groups)
    me = np.arange(groups)
    away = np.minimum(me, groups - 1 - me)
    columns = [me >= groups // 2, away]
    columns += [signs[me, me ^ apart] for apart in range(groups)]
    columns += [1 - 2 * (me >> bit & 1) for bit in range(groups.bit_length() - 1)]
    columns += [away] * KINDS
    table = np.stack(columns, axis=1).astype(np.float32)[:, :, None, None]
    table = jnp.asarray(np.tile(table, (1, 1, 1, length)))
    row = lax.dynamic_index_in_dim(table, lax.axis_index("tensor"), keepdims=False)
    return row[0], row[1], row[2 : 2 + groups], row[2 + groups : -KINDS], row[-KINDS:]


def exchange(block, axis, apart):
    count = lax.axis_size(axis)
    return lax.ppermute(block, axis, [(i, i ^ apart) for i in range(count)])


def spread(block):
    return [block] + [exchange(block, "tensor", k) for k in range(1, lax.axis_size("tensor"))]


def turn(block):
    width = block.shape[-1]
    square = jnp.asarray(sylvester(width), BF16)
    rows = block.reshape(-1, width) * (1.0 / math.sqrt(D))
    high = lax.reduce_precision(rows, 8, 7)
    low = (rows - high).astype(BF16)
    return (dot(high.astype(BF16), square, 1, 0) + dot(low, square, 1, 0)).reshape(block.shape)


def rotate(pieces, signs):
    width = pieces[0].shape[-1]
    return turn(sum(piece.astype(F32) * sign[:, :width] for piece, sign in zip(pieces, signs)))


def rotate_by_halves(block, bits, ahead):
    block = turn(block)
    for level, bit in enumerate(bits):
        message = block.astype(BF16)
        came = exchange(message if level else after(message, ahead), "tensor", 1 << level)
        block = block * bit[:, : block.shape[-1]] + came.astype(F32)
    return block


def dp_stages():
    bits = [1 << bit for bit in reversed(range(lax.axis_size("dp").bit_length() - 1))]
    stages = []
    while len(bits) > 1:
        high, low, bits = bits[0], bits[1], bits[2:]
        stages.append([0, low, high, high | low])
    if bits:
        stages.append([0, bits[0]])
    return stages


def gather_dp(block, axis, ahead):
    stages = dp_stages()
    for stage in stages[:-1]:
        came = [exchange(block, "dp", apart) for apart in stage[1:]]
        for other in ahead:
            block = after(block, other)
        block = jnp.concatenate([block] + came, axis=axis)
    return block, exchange(block, "dp", stages[-1][1])


def scatter_dp(low, high):
    stages = dp_stages()
    first = exchange(high, "dp", stages[-1][1])
    low, came = low + first.astype(F32), first
    for stage in reversed(stages[:-1]):
        low = low.reshape(low.shape[:2] + (len(stage), -1) + low.shape[-1:])
        total = low[:, :, 0]
        for place, apart in enumerate(stage[1:], 1):
            came = exchange(low[:, :, place].astype(BF16), "dp", apart)
            total = total + came.astype(F32)
        low = total
    return low, first, came


def line_pairs(step):
    last = lax.axis_size("tensor") - 1
    return [(step, step + 1), (last - step, last - step - 1)]


def fold_steps():
    return range(lax.axis_size("tensor") // 2 - 1)


def inward(own):
    total = own
    for step in fold_steps()[:-1]:
        came = lax.ppermute(total, "tensor", line_pairs(step))
        total = (total.astype(F32) + came.astype(F32)).astype(BF16)
    return total


def outward(block, depth):
    for step in reversed(fold_steps()[:-1]):
        came = lax.ppermute(block, "tensor", [(b, a) for a, b in line_pairs(step)])
        block = jnp.where(depth[:, : block.shape[-1]] == step, came, block)
    return block


def swap(into, out, depth):
    if not fold_steps():
        return jnp.zeros_like(into if out is None else out)
    inner = len(fold_steps()) - 1
    pairs = line_pairs(inner)
    back = [(b, a) for a, b in pairs]
    if out is None:
        return lax.ppermute(into, "tensor", pairs)
    if into is None:
        return lax.ppermute(out, "tensor", back)
    block = jnp.where(depth[:, : out.shape[-1]] > inner, out, into)
    return lax.ppermute(block, "tensor", pairs + back)


def across(block):
    half = lax.axis_size("tensor") // 2
    return lax.ppermute(block, "tensor", [(half - 1, half), (half, half - 1)])


def activations(gate, up, grad_hidden):
    sigma = jax.nn.sigmoid(gate)
    silu = gate * sigma
    return jnp.stack(
        [
            silu * up,
            grad_hidden * up * sigma * (1.0 + gate * (1.0 - sigma)),
            grad_hidden * silu,
        ]
    ).astype(BF16)


def shards(tokens, gate_weight, up_weight, down_weight, out_grad):
    mine, width = tokens.shape
    peers = lax.axis_size("dp")
    step = STEP if mine % STEP == 0 else mine
    chunks = mine // step
    half = peers * step // 2
    far, depth, signs, bits, depths = my_row(max(width, gate_weight.shape[1]))
    far = far[:, :width] > 0.5

    both = jnp.stack([tokens, out_grad])

    def arrive(turned, ahead=()):
        low, high = gather_dp(turned.reshape(2, -1, 1, step, width), 2, ahead)
        other, own = jnp.where(far, low, high), jnp.where(far, high, low)
        return [part.reshape(2, -1, half, width) for part in (other, own)]

    first = min(2, chunks)
    early = spread(both[:, : first * step])
    late = spread(after(both[:, first * step :], early[1])) if chunks > first else None
    groups = [arrive(rotate(early, signs).astype(BF16))]

    def leave(blocks):
        sums = []
        for block in blocks:
            mixed = dot(block[0], down_weight, 1, 0)
            grads = dot(block[1], gate_weight, 1, 1) + dot(block[2], up_weight, 1, 1)
            sums.append(jnp.stack([mixed, grads]))
        sums = jnp.concatenate(sums, axis=1).reshape(2, -1, 2, half, width)
        low = jnp.where(far, sums[:, :, 0], sums[:, :, 1])
        return low, jnp.where(far, sums[:, :, 1], sums[:, :, 0]).astype(BF16)

    def done(i):
        parts = []
        for k in (2 * i + 1, 2 * i):
            inner = depth[:, : outs[k].shape[-1]] > len(fold_steps()) - 1
            parts.append(outward(jnp.where(inner, outs[k], came[k + LAG]), depth))
        return jnp.concatenate(parts, axis=1)

    steps = 2 * chunks
    split, ends = max(chunks - 2, 0), []
    messages, came, crossed, acts, outs = [], [], [], [], []
    for s in range(steps + LAG):
        if s < steps:
            i, which = divmod(s, 2)
            group, place = (groups[0], i) if i < first else (groups[1], i - first)
            x, g = group[which][0, place], group[which][1, place]
            if s > 0:
                other = acts[i - 2] if i > 3 else came[max(s - LAG, 0)] if s > 1 else messages[0][2:]
                x, g = after(x, other), after(g, other)
            parts = [dot(x, gate_weight, 1, 0), dot(x, up_weight, 1, 0), dot(g, down_weight, 1, 1)]
            message = jnp.stack(parts).astype(BF16)
            messages.append(inward(after(message, came[0]) if s == 1 else message))
        if s == steps + LAG - 1 and split > 0:
            low, high = leave([done(i) for i in range(split)])
            first_sums, ahead, _ = scatter_dp(low, high)
            outs[-1] = after(outs[-1], ahead)
        came.append(
            swap(
                messages[s] if s < steps else None,
                outs[s - LAG] if s >= LAG else None,
                depths[s % KINDS],
            )
        )
        if s == 0 and chunks > first:
            tick = exchange(message[2, :step, :width], "dp", 1)
            late[0] = after(late[0], tick)
        if s == 1 and chunks > first:
            groups.append(arrive(rotate(late, signs).astype(BF16), [messages[1], middle]))
        if s < steps:
            total = messages[s].astype(F32) + came[s].astype(F32)
            if which == 0:
                middle = total.astype(BF16)
                other_sums = across(middle)
            else:
                gate, up, grad_hidden = total + other_sums.astype(F32)
                acts.append(activations(gate, up, grad_hidden))
                crossed.append(across(acts[i]))
                outs += [acts[i], crossed[i]]
    low, high = leave([done(i) for i in range(split, chunks)])
    if split > 0:
        ends.append(rotate_by_halves(first_sums.reshape(2, -1, width), bits, crossed[-1]))
    sums, _, ahead = scatter_dp(low, high)
    ends.append(rotate(spread(sums.reshape(2, -1, width).astype(BF16)), signs))
    ends = jnp.concatenate(ends, axis=1)

    acts = jnp.concatenate([done(i) for i in range(chunks)], axis=1)
    rows = [jnp.stack(group, axis=2).reshape(2, -1, width) for group in groups]
    rows = after(jnp.concatenate(rows, axis=1), high[0, 0, :1])
    late_rows = after(rows[0], ahead[0, 0, :1])
    factor = 1.0 / math.sqrt(rows.shape[1])
    return (
        ends[0],
        ends[1],
        (dot(late_rows, acts[1], 0, 0) * factor).astype(BF16),
        (dot(late_rows, acts[2], 0, 0) * factor).astype(BF16),
        (dot(acts[0], rows[1], 0, 0) * factor).astype(BF16),
    )


def solution(mesh):
    return jax.shard_map(
        shards,
        mesh=mesh,
        in_specs=(
            P("dp", "tensor"),
            P("tensor", "dp"),
            P("tensor", "dp"),
            P("dp", "tensor"),
            P("dp", "tensor"),
        ),
        out_specs=(
            P("dp", "tensor"),
            P("dp", "tensor"),
            P("tensor", "dp"),
            P("tensor", "dp"),
            P("dp", "tensor"),
        ),
        check_vma=False,
    )
```

```python
import math

import jax
import jax.numpy as jnp
import numpy as np
from jax import lax
from jax.sharding import PartitionSpec as P

D = 2048
BF16 = jnp.bfloat16
F32 = jnp.float32
STEP = 16
LAG = 3
KINDS = 4


def sylvester(order):
    table = np.ones((1, 1), np.float32)
    while table.shape[0] < order:
        table = np.block([[table, table], [table, -table]])
    return table


def dot(left, right, left_dim, right_dim):
    return lax.dot_general(
        left, right, (((left_dim,), (right_dim,)), ((), ())), preferred_element_type=F32
    )


def after(block, other):
    other = other.reshape((-1,) + other.shape[-2:])[0]
    if other.shape[0] < block.shape[-2]:
        other = other[:1]
    other = other[: block.shape[-2]]
    wide = block.shape[-1]
    if other.shape[-1] < wide:
        other = jnp.concatenate([other] * (-(-wide // other.shape[-1])), axis=-1)
    other = other[:, :wide].astype(block.dtype)
    return jnp.where(jnp.isnan(other), other, block)


def my_row(length):
    groups = lax.axis_size("tensor")
    signs = sylvester(groups)
    me = np.arange(groups)
    away = np.minimum(me, groups - 1 - me)
    columns = [me >= groups // 2, away]
    columns += [signs[me, me ^ apart] for apart in range(groups)]
    columns += [1 - 2 * (me >> bit & 1) for bit in range(groups.bit_length() - 1)]
    columns += [away] * KINDS
    table = np.stack(columns, axis=1).astype(np.float32)[:, :, None, None]
    table = jnp.asarray(np.tile(table, (1, 1, 1, length)))
    row = lax.dynamic_index_in_dim(table, lax.axis_index("tensor"), keepdims=False)
    return row[0], row[1], row[2 : 2 + groups], row[2 + groups : -KINDS], row[-KINDS:]


def exchange(block, axis, apart):
    count = lax.axis_size(axis)
    return lax.ppermute(block, axis, [(i, i ^ apart) for i in range(count)])


def spread(block):
    return [block] + [exchange(block, "tensor", k) for k in range(1, lax.axis_size("tensor"))]


def turn(block):
    width = block.shape[-1]
    square = jnp.asarray(sylvester(width), BF16)
    rows = block.reshape(-1, width) * (1.0 / math.sqrt(D))
    high = lax.reduce_precision(rows, 8, 7)
    low = (rows - high).astype(BF16)
    return (dot(high.astype(BF16), square, 1, 0) + dot(low, square, 1, 0)).reshape(block.shape)


def rotate(pieces, signs):
    width = pieces[0].shape[-1]
    return turn(sum(piece.astype(F32) * sign[:, :width] for piece, sign in zip(pieces, signs)))


def rotate_by_halves(block, bits, ahead):
    block = turn(block)
    for level, bit in enumerate(bits):
        message = block.astype(BF16)
        came = exchange(after(message, ahead[level]) if level < len(ahead) else message, "tensor", 1 << level)
        block = block * bit[:, : block.shape[-1]] + came.astype(F32)
    return block


def dp_stages():
    bits = [1 << bit for bit in reversed(range(lax.axis_size("dp").bit_length() - 1))]
    stages = []
    while len(bits) > 1:
        high, low, bits = bits[0], bits[1], bits[2:]
        stages.append([0, low, high, high | low])
    if bits:
        stages.append([0, bits[0]])
    return stages


def gather_dp(block, axis, ahead):
    stages = dp_stages()
    for stage in stages[:-1]:
        came = [exchange(block, "dp", apart) for apart in stage[1:]]
        for other in ahead:
            block = after(block, other)
        block = jnp.concatenate([block] + came, axis=axis)
    return block, exchange(block, "dp", stages[-1][1])


def scatter_dp(low, high):
    stages = dp_stages()
    first = exchange(high, "dp", stages[-1][1])
    low, came = low + first.astype(F32), first
    for stage in reversed(stages[:-1]):
        low = low.reshape(low.shape[:2] + (len(stage), -1) + low.shape[-1:])
        total = low[:, :, 0]
        for place, apart in enumerate(stage[1:], 1):
            came = exchange(low[:, :, place].astype(BF16), "dp", apart)
            total = total + came.astype(F32)
        low = total
    return low, first, came


def line_pairs(step):
    last = lax.axis_size("tensor") - 1
    return [(step, step + 1), (last - step, last - step - 1)]


def fold_steps():
    return range(lax.axis_size("tensor") // 2 - 1)


def inward(own):
    total = own
    for step in fold_steps()[:-1]:
        came = lax.ppermute(total, "tensor", line_pairs(step))
        total = (total.astype(F32) + came.astype(F32)).astype(BF16)
    return total


def outward(block, depth):
    for step in reversed(fold_steps()[:-1]):
        came = lax.ppermute(block, "tensor", [(b, a) for a, b in line_pairs(step)])
        block = jnp.where(depth[:, : block.shape[-1]] == step, came, block)
    return block


def swap(into, out, depth):
    if not fold_steps():
        return jnp.zeros_like(into if out is None else out)
    inner = len(fold_steps()) - 1
    pairs = line_pairs(inner)
    back = [(b, a) for a, b in pairs]
    if out is None:
        return lax.ppermute(into, "tensor", pairs)
    if into is None:
        return lax.ppermute(out, "tensor", back)
    block = jnp.where(depth[:, : out.shape[-1]] > inner, out, into)
    return lax.ppermute(block, "tensor", pairs + back)


def across(block):
    half = lax.axis_size("tensor") // 2
    return lax.ppermute(block, "tensor", [(half - 1, half), (half, half - 1)])


def activations(gate, up, grad_hidden):
    sigma = jax.nn.sigmoid(gate)
    silu = gate * sigma
    return jnp.stack(
        [
            silu * up,
            grad_hidden * up * sigma * (1.0 + gate * (1.0 - sigma)),
            grad_hidden * silu,
        ]
    ).astype(BF16)


def shards(tokens, gate_weight, up_weight, down_weight, out_grad):
    mine, width = tokens.shape
    peers = lax.axis_size("dp")
    step = STEP if mine % STEP == 0 else mine
    chunks = mine // step
    half = peers * step // 2
    far, depth, signs, bits, depths = my_row(max(width, gate_weight.shape[1]))
    far = far[:, :width] > 0.5

    both = jnp.stack([tokens, out_grad])

    def arrive(turned, ahead=()):
        low, high = gather_dp(turned.reshape(2, -1, 1, step, width), 2, ahead)
        other, own = jnp.where(far, low, high), jnp.where(far, high, low)
        return [part.reshape(2, -1, half, width) for part in (other, own)]

    first = min(2, chunks)
    early = spread(both[:, : first * step])
    late = spread(after(both[:, first * step :], early[1])) if chunks > first else None
    groups = [arrive(rotate(early, signs).astype(BF16))]

    def leave(blocks):
        sums = []
        for block in blocks:
            mixed = dot(block[0], down_weight, 1, 0)
            grads = dot(block[1], gate_weight, 1, 1) + dot(block[2], up_weight, 1, 1)
            sums.append(jnp.stack([mixed, grads]))
        sums = jnp.concatenate(sums, axis=1).reshape(2, -1, 2, half, width)
        low = jnp.where(far, sums[:, :, 0], sums[:, :, 1])
        return low, jnp.where(far, sums[:, :, 1], sums[:, :, 0]).astype(BF16)

    def done(i):
        parts = []
        for k in (2 * i + 1, 2 * i):
            inner = depth[:, : outs[k].shape[-1]] > len(fold_steps()) - 1
            parts.append(outward(jnp.where(inner, outs[k], came[k + LAG]), depth))
        return jnp.concatenate(parts, axis=1)

    steps = 2 * chunks
    split, ends = max(chunks - 2, 0), []
    messages, came, crossed, acts, outs = [], [], [], [], []
    for s in range(steps + LAG):
        if s < steps:
            i, which = divmod(s, 2)
            group, place = (groups[0], i) if i < first else (groups[1], i - first)
            x, g = group[which][0, place], group[which][1, place]
            if s > 0:
                other = acts[i - 2] if i > 3 else came[max(s - LAG, 0)] if s > 1 else messages[0][2:]
                x, g = after(x, other), after(g, other)
            parts = [dot(x, gate_weight, 1, 0), dot(x, up_weight, 1, 0), dot(g, down_weight, 1, 1)]
            message = jnp.stack(parts).astype(BF16)
            messages.append(inward(after(message, came[0]) if s == 1 else message))
        if s == steps + LAG - 1 and split > 0:
            low, high = leave([done(i) for i in range(split)])
            first_sums, ahead, _ = scatter_dp(low, high)
            outs[-1] = after(outs[-1], ahead)
        came.append(
            swap(
                messages[s] if s < steps else None,
                outs[s - LAG] if s >= LAG else None,
                depths[s % KINDS],
            )
        )
        if s == 0 and chunks > first:
            tick = exchange(message[2, :step, :width], "dp", 1)
            late[0] = after(late[0], tick)
        if s == 1 and chunks > first:
            groups.append(arrive(rotate(late, signs).astype(BF16), [messages[1], middle]))
        if s < steps:
            total = messages[s].astype(F32) + came[s].astype(F32)
            if which == 0:
                middle = total.astype(BF16)
                other_sums = across(middle)
            else:
                gate, up, grad_hidden = total + other_sums.astype(F32)
                acts.append(activations(gate, up, grad_hidden))
                crossed.append(across(acts[i]))
                outs += [acts[i], crossed[i]]
    low, high = leave([done(i) for i in range(split, chunks)])
    sums, _, ahead = scatter_dp(low, high)
    if split > 0:
        first_sums = first_sums.reshape(2, -1, width)
        ends.append(rotate_by_halves(first_sums, bits, [came[-1], ahead]))
    ends.append(rotate(spread(sums.reshape(2, -1, width).astype(BF16)), signs))
    ends = jnp.concatenate(ends, axis=1)

    acts = jnp.concatenate([done(i) for i in range(chunks)], axis=1)
    rows = [jnp.stack(group, axis=2).reshape(2, -1, width) for group in groups]
    rows = after(jnp.concatenate(rows, axis=1), high[0, 0, :1])
    late_rows = after(rows[0], ahead[0, 0, :1])
    factor = 1.0 / math.sqrt(rows.shape[1])
    return (
        ends[0],
        ends[1],
        (dot(late_rows, acts[1], 0, 0) * factor).astype(BF16),
        (dot(late_rows, acts[2], 0, 0) * factor).astype(BF16),
        (dot(acts[0], rows[1], 0, 0) * factor).astype(BF16),
    )


def solution(mesh):
    return jax.shard_map(
        shards,
        mesh=mesh,
        in_specs=(
            P("dp", "tensor"),
            P("tensor", "dp"),
            P("tensor", "dp"),
            P("dp", "tensor"),
            P("dp", "tensor"),
        ),
        out_specs=(
            P("dp", "tensor"),
            P("dp", "tensor"),
            P("tensor", "dp"),
            P("tensor", "dp"),
            P("dp", "tensor"),
        ),
        check_vma=False,
    )
```

```python
import math

import jax
import jax.numpy as jnp
import numpy as np
from jax import lax
from jax.sharding import PartitionSpec as P

D = 2048
BF16 = jnp.bfloat16
F32 = jnp.float32
STEP = 16
LAG = 3
KINDS = 4


def sylvester(order):
    table = np.ones((1, 1), np.float32)
    while table.shape[0] < order:
        table = np.block([[table, table], [table, -table]])
    return table


def signs_of(order, ahead):
    shape = (order, order)
    common = lax.broadcasted_iota(jnp.int32, shape, 0) & lax.broadcasted_iota(jnp.int32, shape, 1)
    shift = 1
    while shift < order.bit_length():
        shift *= 2
    while shift > 1:
        shift //= 2
        common = common ^ (common >> shift)
    return lax.optimization_barrier(after((1 - 2 * (common & 1)).astype(BF16), ahead))


def dot(left, right, left_dim, right_dim):
    return lax.dot_general(
        left, right, (((left_dim,), (right_dim,)), ((), ())), preferred_element_type=F32
    )


def after(block, other):
    other = other.reshape((-1,) + other.shape[-2:])[0]
    if other.shape[0] < block.shape[-2]:
        other = other[:1]
    other = other[: block.shape[-2]]
    wide = block.shape[-1]
    if other.shape[-1] < wide:
        other = jnp.concatenate([other] * (-(-wide // other.shape[-1])), axis=-1)
    other = other[:, :wide].astype(block.dtype)
    return jnp.where(jnp.isnan(other), other, block)


def my_row(length):
    groups = lax.axis_size("tensor")
    signs = sylvester(groups)
    me = np.arange(groups)
    away = np.minimum(me, groups - 1 - me)
    columns = [me >= groups // 2, away]
    columns += [signs[me, me ^ apart] for apart in range(groups)]
    columns += [1 - 2 * (me >> bit & 1) for bit in range(groups.bit_length() - 1)]
    columns += [away] * KINDS
    table = np.stack(columns, axis=1).astype(np.float32)[:, :, None, None]
    table = jnp.asarray(np.tile(table, (1, 1, 1, length)))
    row = lax.dynamic_index_in_dim(table, lax.axis_index("tensor"), keepdims=False)
    return row[0], row[1], row[2 : 2 + groups], row[2 + groups : -KINDS], row[-KINDS:]


def exchange(block, axis, apart):
    count = lax.axis_size(axis)
    return lax.ppermute(block, axis, [(i, i ^ apart) for i in range(count)])


def spread(block):
    return [block] + [exchange(block, "tensor", k) for k in range(1, lax.axis_size("tensor"))]


def turn(block, square):
    width = block.shape[-1]
    rows = block.reshape(-1, width) * (1.0 / math.sqrt(D))
    high = lax.reduce_precision(rows, 8, 7)
    low = (rows - high).astype(BF16)
    return (dot(high.astype(BF16), square, 1, 0) + dot(low, square, 1, 0)).reshape(block.shape)


def rotate(pieces, signs, square):
    width = pieces[0].shape[-1]
    return turn(sum(piece.astype(F32) * sign[:, :width] for piece, sign in zip(pieces, signs)), square)


def rotate_by_halves(block, bits, square):
    block = turn(block, square)
    for level, bit in enumerate(bits):
        came = exchange(block.astype(BF16), "tensor", 1 << level)
        block = block * bit[:, : block.shape[-1]] + came.astype(F32)
    return block


def dp_stages():
    bits = [1 << bit for bit in reversed(range(lax.axis_size("dp").bit_length() - 1))]
    stages = []
    while len(bits) > 1:
        high, low, bits = bits[0], bits[1], bits[2:]
        stages.append([0, low, high, high | low])
    if bits:
        stages.append([0, bits[0]])
    return stages


def gather_dp(block, axis, ahead):
    stages = dp_stages()
    for stage in stages[:-1]:
        came = [exchange(block, "dp", apart) for apart in stage[1:]]
        for other in ahead:
            block = after(block, other)
        block = jnp.concatenate([block] + came, axis=axis)
    return block, exchange(block, "dp", stages[-1][1])


def scatter_dp(low, high):
    stages = dp_stages()
    first = exchange(high, "dp", stages[-1][1])
    low, came = low + first.astype(F32), first
    for stage in reversed(stages[:-1]):
        low = low.reshape(low.shape[:2] + (len(stage), -1) + low.shape[-1:])
        total = low[:, :, 0]
        for place, apart in enumerate(stage[1:], 1):
            came = exchange(low[:, :, place].astype(BF16), "dp", apart)
            total = total + came.astype(F32)
        low = total
    return low, first, came


def line_pairs(step):
    last = lax.axis_size("tensor") - 1
    return [(step, step + 1), (last - step, last - step - 1)]


def fold_steps():
    return range(lax.axis_size("tensor") // 2 - 1)


def inward(own):
    total = own
    for step in fold_steps()[:-1]:
        came = lax.ppermute(total, "tensor", line_pairs(step))
        total = (total.astype(F32) + came.astype(F32)).astype(BF16)
    return total


def outward(block, depth):
    for step in reversed(fold_steps()[:-1]):
        came = lax.ppermute(block, "tensor", [(b, a) for a, b in line_pairs(step)])
        block = jnp.where(depth[:, : block.shape[-1]] == step, came, block)
    return block


def swap(into, out, depth):
    if not fold_steps():
        return jnp.zeros_like(into if out is None else out)
    inner = len(fold_steps()) - 1
    pairs = line_pairs(inner)
    back = [(b, a) for a, b in pairs]
    if out is None:
        return lax.ppermute(into, "tensor", pairs)
    if into is None:
        return lax.ppermute(out, "tensor", back)
    block = jnp.where(depth[:, : out.shape[-1]] > inner, out, into)
    return lax.ppermute(block, "tensor", pairs + back)


def across(block):
    half = lax.axis_size("tensor") // 2
    return lax.ppermute(block, "tensor", [(half - 1, half), (half, half - 1)])


def activations(gate, up, grad_hidden):
    sigma = jax.nn.sigmoid(gate)
    silu = gate * sigma
    return jnp.stack(
        [
            silu * up,
            grad_hidden * up * sigma * (1.0 + gate * (1.0 - sigma)),
            grad_hidden * silu,
        ]
    ).astype(BF16)


def shards(tokens, gate_weight, up_weight, down_weight, out_grad):
    mine, width = tokens.shape
    peers = lax.axis_size("dp")
    step = STEP if mine % STEP == 0 else mine
    chunks = mine // step
    half = peers * step // 2
    far, depth, signs, bits, depths = my_row(max(width, gate_weight.shape[1]))
    far = far[:, :width] > 0.5

    square = signs_of(width, depth)
    both = jnp.stack([tokens, out_grad])

    def arrive(turned, ahead=()):
        low, high = gather_dp(turned.reshape(2, -1, 1, step, width), 2, ahead)
        other, own = jnp.where(far, low, high), jnp.where(far, high, low)
        return [part.reshape(2, -1, half, width) for part in (other, own)]

    first = min(2, chunks)
    early = spread(both[:, : first * step])
    late = spread(after(both[:, first * step :], early[1])) if chunks > first else None
    groups = [arrive(rotate(early, signs, square).astype(BF16))]

    def leave(blocks):
        sums = []
        for block in blocks:
            mixed = dot(block[0], down_weight, 1, 0)
            grads = dot(block[1], gate_weight, 1, 1) + dot(block[2], up_weight, 1, 1)
            sums.append(jnp.stack([mixed, grads]))
        sums = jnp.concatenate(sums, axis=1).reshape(2, -1, 2, half, width)
        low = jnp.where(far, sums[:, :, 0], sums[:, :, 1])
        return low, jnp.where(far, sums[:, :, 1], sums[:, :, 0]).astype(BF16)

    def done(i):
        parts = []
        for k in (2 * i + 1, 2 * i):
            inner = depth[:, : outs[k].shape[-1]] > len(fold_steps()) - 1
            parts.append(outward(jnp.where(inner, outs[k], came[k + LAG]), depth))
        return jnp.concatenate(parts, axis=1)

    steps = 2 * chunks
    split, ends = max(chunks - 2, 0), []
    messages, came, crossed, acts, outs = [], [], [], [], []
    for s in range(steps + LAG):
        if s < steps:
            i, which = divmod(s, 2)
            group, place = (groups[0], i) if i < first else (groups[1], i - first)
            x, g = group[which][0, place], group[which][1, place]
            if s > 0:
                other = acts[i - 2] if i > 3 else came[max(s - LAG, 0)] if s > 1 else messages[0][2:]
                x, g = after(x, other), after(g, other)
            parts = [dot(x, gate_weight, 1, 0), dot(x, up_weight, 1, 0), dot(g, down_weight, 1, 1)]
            message = jnp.stack(parts).astype(BF16)
            messages.append(inward(after(message, came[0]) if s == 1 else message))
        if s == steps + LAG - 1 and split > 0:
            low, high = leave([done(i) for i in range(split)])
            first_sums, ahead, _ = scatter_dp(low, high)
            outs[-1] = after(outs[-1], ahead)
        came.append(
            swap(
                messages[s] if s < steps else None,
                outs[s - LAG] if s >= LAG else None,
                depths[s % KINDS],
            )
        )
        if s == 0 and chunks > first:
            tick = exchange(message[2, :step, :width], "dp", 1)
            late[0] = after(late[0], tick)
        if s == 1 and chunks > first:
            groups.append(arrive(rotate(late, signs, square).astype(BF16), [messages[1], middle]))
        if s < steps:
            total = messages[s].astype(F32) + came[s].astype(F32)
            if which == 0:
                middle = total.astype(BF16)
                other_sums = across(middle)
            else:
                gate, up, grad_hidden = total + other_sums.astype(F32)
                acts.append(activations(gate, up, grad_hidden))
                crossed.append(across(acts[i]))
                outs += [acts[i], crossed[i]]
    low, high = leave([done(i) for i in range(split, chunks)])
    if split > 0:
        first_sums = after(first_sums.reshape(2, -1, width), came[-1])
        ends.append(rotate_by_halves(first_sums, bits, square))
    sums, _, ahead = scatter_dp(low, high)
    ends.append(rotate(spread(sums.reshape(2, -1, width).astype(BF16)), signs, square))
    ends = jnp.concatenate(ends, axis=1)

    acts = jnp.concatenate([done(i) for i in range(chunks)], axis=1)
    rows = [jnp.stack(group, axis=2).reshape(2, -1, width) for group in groups]
    rows = after(jnp.concatenate(rows, axis=1), high[0, 0, :1])
    late_rows = after(rows[0], ahead[0, 0, :1])
    factor = 1.0 / math.sqrt(rows.shape[1])
    return (
        ends[0],
        ends[1],
        (dot(late_rows, acts[1], 0, 0) * factor).astype(BF16),
        (dot(late_rows, acts[2], 0, 0) * factor).astype(BF16),
        (dot(acts[0], rows[1], 0, 0) * factor).astype(BF16),
    )


def solution(mesh):
    return jax.shard_map(
        shards,
        mesh=mesh,
        in_specs=(
            P("dp", "tensor"),
            P("tensor", "dp"),
            P("tensor", "dp"),
            P("dp", "tensor"),
            P("dp", "tensor"),
        ),
        out_specs=(
            P("dp", "tensor"),
            P("dp", "tensor"),
            P("tensor", "dp"),
            P("tensor", "dp"),
            P("dp", "tensor"),
        ),
        check_vma=False,
    )
```

```python
import math

import jax
import jax.numpy as jnp
import numpy as np
from jax import lax
from jax.sharding import PartitionSpec as P

D = 2048
BF16 = jnp.bfloat16
F32 = jnp.float32
STEP = 16
LAG = 3
KINDS = 4


def sylvester(order):
    table = np.ones((1, 1), np.float32)
    while table.shape[0] < order:
        table = np.block([[table, table], [table, -table]])
    return table


def signs_of(order, ahead):
    shape = (order, order)
    common = lax.broadcasted_iota(jnp.int32, shape, 0) & lax.broadcasted_iota(jnp.int32, shape, 1)
    shift = 1
    while shift < order.bit_length():
        shift *= 2
    while shift > 1:
        shift //= 2
        common = common ^ (common >> shift)
    return lax.optimization_barrier(after((1 - 2 * (common & 1)).astype(BF16), ahead))


def dot(left, right, left_dim, right_dim):
    return lax.dot_general(
        left, right, (((left_dim,), (right_dim,)), ((), ())), preferred_element_type=F32
    )


def after(block, other):
    other = other.reshape((-1,) + other.shape[-2:])[0]
    if other.shape[0] < block.shape[-2]:
        other = other[:1]
    other = other[: block.shape[-2]]
    wide = block.shape[-1]
    if other.shape[-1] < wide:
        other = jnp.concatenate([other] * (-(-wide // other.shape[-1])), axis=-1)
    other = other[:, :wide].astype(block.dtype)
    return jnp.where(jnp.isnan(other), other, block)


def my_row(length):
    groups = lax.axis_size("tensor")
    signs = sylvester(groups)
    me = np.arange(groups)
    away = np.minimum(me, groups - 1 - me)
    columns = [me >= groups // 2, away]
    columns += [signs[me, me ^ apart] for apart in range(groups)]
    columns += [1 - 2 * (me >> bit & 1) for bit in range(groups.bit_length() - 1)]
    columns += [away] * KINDS
    table = np.stack(columns, axis=1).astype(np.float32)[:, :, None, None]
    table = jnp.asarray(np.tile(table, (1, 1, 1, length)))
    row = lax.dynamic_index_in_dim(table, lax.axis_index("tensor"), keepdims=False)
    return row[0], row[1], row[2 : 2 + groups], row[2 + groups : -KINDS], row[-KINDS:]


def exchange(block, axis, apart):
    count = lax.axis_size(axis)
    return lax.ppermute(block, axis, [(i, i ^ apart) for i in range(count)])


def spread(block):
    return [block] + [exchange(block, "tensor", k) for k in range(1, lax.axis_size("tensor"))]


def turn(block, square):
    width = block.shape[-1]
    rows = block.reshape(-1, width) * (1.0 / math.sqrt(D))
    high = lax.reduce_precision(rows, 8, 7)
    low = (rows - high).astype(BF16)
    return (dot(high.astype(BF16), square, 1, 0) + dot(low, square, 1, 0)).reshape(block.shape)


def rotate(pieces, signs, square):
    width = pieces[0].shape[-1]
    return turn(sum(piece.astype(F32) * sign[:, :width] for piece, sign in zip(pieces, signs)), square)


def rotate_by_halves(block, bits, square, ahead):
    block = turn(block, square)
    for level, bit in enumerate(bits):
        message = block.astype(BF16)
        message = after(message, ahead) if level else message
        came = exchange(message, "tensor", 1 << level)
        block = block * bit[:, : block.shape[-1]] + came.astype(F32)
    return block, message


def dp_stages():
    bits = [1 << bit for bit in reversed(range(lax.axis_size("dp").bit_length() - 1))]
    stages = []
    while len(bits) > 1:
        high, low, bits = bits[0], bits[1], bits[2:]
        stages.append([0, low, high, high | low])
    if bits:
        stages.append([0, bits[0]])
    return stages


def gather_dp(block, axis, ahead):
    stages = dp_stages()
    for stage in stages[:-1]:
        came = [exchange(block, "dp", apart) for apart in stage[1:]]
        for other in ahead:
            block = after(block, other)
        block = jnp.concatenate([block] + came, axis=axis)
    return block, exchange(block, "dp", stages[-1][1])


def scatter_dp(low, high):
    stages = dp_stages()
    first = exchange(high, "dp", stages[-1][1])
    low, came = low + first.astype(F32), first
    for stage in reversed(stages[:-1]):
        low = low.reshape(low.shape[:2] + (len(stage), -1) + low.shape[-1:])
        total = low[:, :, 0]
        for place, apart in enumerate(stage[1:], 1):
            came = exchange(low[:, :, place].astype(BF16), "dp", apart)
            total = total + came.astype(F32)
        low = total
    return low, first, came


def line_pairs(step):
    last = lax.axis_size("tensor") - 1
    return [(step, step + 1), (last - step, last - step - 1)]


def fold_steps():
    return range(lax.axis_size("tensor") // 2 - 1)


def inward(own):
    total = own
    for step in fold_steps()[:-1]:
        came = lax.ppermute(total, "tensor", line_pairs(step))
        total = (total.astype(F32) + came.astype(F32)).astype(BF16)
    return total


def outward(block, depth):
    for step in reversed(fold_steps()[:-1]):
        came = lax.ppermute(block, "tensor", [(b, a) for a, b in line_pairs(step)])
        block = jnp.where(depth[:, : block.shape[-1]] == step, came, block)
    return block


def swap(into, out, depth):
    if not fold_steps():
        return jnp.zeros_like(into if out is None else out)
    inner = len(fold_steps()) - 1
    pairs = line_pairs(inner)
    back = [(b, a) for a, b in pairs]
    if out is None:
        return lax.ppermute(into, "tensor", pairs)
    if into is None:
        return lax.ppermute(out, "tensor", back)
    block = jnp.where(depth[:, : out.shape[-1]] > inner, out, into)
    return lax.ppermute(block, "tensor", pairs + back)


def across(block):
    half = lax.axis_size("tensor") // 2
    return lax.ppermute(block, "tensor", [(half - 1, half), (half, half - 1)])


def activations(gate, up, grad_hidden):
    sigma = jax.nn.sigmoid(gate)
    silu = gate * sigma
    return jnp.stack(
        [
            silu * up,
            grad_hidden * up * sigma * (1.0 + gate * (1.0 - sigma)),
            grad_hidden * silu,
        ]
    ).astype(BF16)


def shards(tokens, gate_weight, up_weight, down_weight, out_grad):
    mine, width = tokens.shape
    peers = lax.axis_size("dp")
    step = STEP if mine % STEP == 0 else mine
    chunks = mine // step
    half = peers * step // 2
    far, depth, signs, bits, depths = my_row(max(width, gate_weight.shape[1]))
    far = far[:, :width] > 0.5

    square = signs_of(width, depth)
    both = jnp.stack([tokens, out_grad])

    def arrive(turned, ahead=()):
        low, high = gather_dp(turned.reshape(2, -1, 1, step, width), 2, ahead)
        other, own = jnp.where(far, low, high), jnp.where(far, high, low)
        return [part.reshape(2, -1, half, width) for part in (other, own)]

    first = min(2, chunks)
    early = spread(both[:, : first * step])
    late = spread(after(both[:, first * step :], early[1])) if chunks > first else None
    groups = [arrive(rotate(early, signs, square).astype(BF16))]

    def leave(blocks):
        sums = []
        for block in blocks:
            mixed = dot(block[0], down_weight, 1, 0)
            grads = dot(block[1], gate_weight, 1, 1) + dot(block[2], up_weight, 1, 1)
            sums.append(jnp.stack([mixed, grads]))
        sums = jnp.concatenate(sums, axis=1).reshape(2, -1, 2, half, width)
        low = jnp.where(far, sums[:, :, 0], sums[:, :, 1])
        return low, jnp.where(far, sums[:, :, 1], sums[:, :, 0]).astype(BF16)

    def done(i):
        parts = []
        for k in (2 * i + 1, 2 * i):
            inner = depth[:, : outs[k].shape[-1]] > len(fold_steps()) - 1
            parts.append(outward(jnp.where(inner, outs[k], came[k + LAG]), depth))
        return jnp.concatenate(parts, axis=1)

    steps = 2 * chunks
    split, ends = max(chunks - 2, 0), []
    messages, came, crossed, acts, outs = [], [], [], [], []
    for s in range(steps + LAG):
        if s < steps:
            i, which = divmod(s, 2)
            group, place = (groups[0], i) if i < first else (groups[1], i - first)
            x, g = group[which][0, place], group[which][1, place]
            if s > 0:
                other = acts[i - 2] if i > 3 else came[max(s - LAG, 0)] if s > 1 else messages[0][2:]
                x, g = after(x, other), after(g, other)
            parts = [dot(x, gate_weight, 1, 0), dot(x, up_weight, 1, 0), dot(g, down_weight, 1, 1)]
            message = jnp.stack(parts).astype(BF16)
            messages.append(inward(after(message, came[0]) if s == 1 else message))
        if s == steps + LAG - 1 and split > 0:
            low, high = leave([done(i) for i in range(split)])
            first_sums, ahead, _ = scatter_dp(low, high)
            outs[-1] = after(outs[-1], ahead)
        came.append(
            swap(
                messages[s] if s < steps else None,
                outs[s - LAG] if s >= LAG else None,
                depths[s % KINDS],
            )
        )
        if s == 0 and chunks > first:
            tick = exchange(message[2, :step, :width], "dp", 1)
            late[0] = after(late[0], tick)
        if s == 1 and chunks > first:
            groups.append(arrive(rotate(late, signs, square).astype(BF16), [messages[1], middle]))
        if s < steps:
            total = messages[s].astype(F32) + came[s].astype(F32)
            if which == 0:
                middle = total.astype(BF16)
                other_sums = across(middle)
            else:
                gate, up, grad_hidden = total + other_sums.astype(F32)
                acts.append(activations(gate, up, grad_hidden))
                crossed.append(across(acts[i]))
                outs += [acts[i], crossed[i]]
    low, high = leave([done(i) for i in range(split, chunks)])
    sums, _, ahead = scatter_dp(low, high)
    if split > 0:
        first_sums = after(first_sums.reshape(2, -1, width), came[-1])
        block, ahead = rotate_by_halves(first_sums, bits, square, ahead)
        ends.append(block)
    ends.append(rotate(spread(sums.reshape(2, -1, width).astype(BF16)), signs, square))
    ends = jnp.concatenate(ends, axis=1)

    acts = jnp.concatenate([done(i) for i in range(chunks)], axis=1)
    rows = [jnp.stack(group, axis=2).reshape(2, -1, width) for group in groups]
    rows = after(jnp.concatenate(rows, axis=1), high[0, 0, :1])
    late_rows = after(rows[0], ahead.reshape(-1, width)[:1])
    factor = 1.0 / math.sqrt(rows.shape[1])
    return (
        ends[0],
        ends[1],
        (dot(late_rows, acts[1], 0, 0) * factor).astype(BF16),
        (dot(late_rows, acts[2], 0, 0) * factor).astype(BF16),
        (dot(acts[0], rows[1], 0, 0) * factor).astype(BF16),
    )


def solution(mesh):
    return jax.shard_map(
        shards,
        mesh=mesh,
        in_specs=(
            P("dp", "tensor"),
            P("tensor", "dp"),
            P("tensor", "dp"),
            P("dp", "tensor"),
            P("dp", "tensor"),
        ),
        out_specs=(
            P("dp", "tensor"),
            P("dp", "tensor"),
            P("tensor", "dp"),
            P("tensor", "dp"),
            P("dp", "tensor"),
        ),
        check_vma=False,
    )
```

```python
import math

import jax
import jax.numpy as jnp
import numpy as np
from jax import lax
from jax.sharding import PartitionSpec as P

D = 2048
BF16 = jnp.bfloat16
F32 = jnp.float32
STEP = 16
LAG = 3
KINDS = 4


def sylvester(order):
    table = np.ones((1, 1), np.float32)
    while table.shape[0] < order:
        table = np.block([[table, table], [table, -table]])
    return table


def signs_of(order, ahead):
    shape = (order, order)
    common = lax.broadcasted_iota(jnp.int32, shape, 0) & lax.broadcasted_iota(jnp.int32, shape, 1)
    shift = 1
    while shift < order.bit_length():
        shift *= 2
    while shift > 1:
        shift //= 2
        common = common ^ (common >> shift)
    return lax.optimization_barrier(after((1 - 2 * (common & 1)).astype(BF16), ahead))


def dot(left, right, left_dim, right_dim):
    return lax.dot_general(
        left, right, (((left_dim,), (right_dim,)), ((), ())), preferred_element_type=F32
    )


def after(block, other):
    other = other.reshape((-1,) + other.shape[-2:])[0]
    if other.shape[0] < block.shape[-2]:
        other = other[:1]
    other = other[: block.shape[-2]]
    wide = block.shape[-1]
    if other.shape[-1] < wide:
        other = jnp.concatenate([other] * (-(-wide // other.shape[-1])), axis=-1)
    other = other[:, :wide].astype(block.dtype)
    return jnp.where(jnp.isnan(other), other, block)


def my_row(length):
    groups = lax.axis_size("tensor")
    signs = sylvester(groups)
    me = np.arange(groups)
    away = np.minimum(me, groups - 1 - me)
    columns = [me >= groups // 2, away]
    columns += [signs[me, me ^ apart] for apart in range(groups)]
    columns += [1 - 2 * (me >> bit & 1) for bit in range(groups.bit_length() - 1)]
    columns += [away] * KINDS
    table = np.stack(columns, axis=1).astype(np.float32)[:, :, None, None]
    table = jnp.asarray(np.tile(table, (1, 1, 1, length)))
    row = lax.dynamic_index_in_dim(table, lax.axis_index("tensor"), keepdims=False)
    return row[0], row[1], row[2 : 2 + groups], row[2 + groups : -KINDS], row[-KINDS:]


def exchange(block, axis, apart):
    count = lax.axis_size(axis)
    return lax.ppermute(block, axis, [(i, i ^ apart) for i in range(count)])


def spread(block):
    return [block] + [exchange(block, "tensor", k) for k in range(1, lax.axis_size("tensor"))]


def turn(block, square):
    width = block.shape[-1]
    rows = block.reshape(-1, width) * (1.0 / math.sqrt(D))
    high = lax.reduce_precision(rows, 8, 7)
    low = (rows - high).astype(BF16)
    return (dot(high.astype(BF16), square, 1, 0) + dot(low, square, 1, 0)).reshape(block.shape)


def rotate(pieces, signs, square):
    width = pieces[0].shape[-1]
    return turn(sum(piece.astype(F32) * sign[:, :width] for piece, sign in zip(pieces, signs)), square)


def rotate_by_halves(block, bits, square, ahead):
    block = turn(block, square)
    for level, bit in enumerate(bits):
        message = block.astype(BF16)
        message = after(message, ahead) if level else message
        came = exchange(message, "tensor", 1 << level)
        block = block * bit[:, : block.shape[-1]] + came.astype(F32)
    return block, message


def dp_stages():
    bits = [1 << bit for bit in reversed(range(lax.axis_size("dp").bit_length() - 1))]
    stages = []
    while len(bits) > 1:
        high, low, bits = bits[0], bits[1], bits[2:]
        stages.append([0, low, high, high | low])
    if bits:
        stages.append([0, bits[0]])
    return stages


def gather_dp(block, axis, ahead):
    stages = dp_stages()
    for stage in stages[:-1]:
        came = [exchange(block, "dp", apart) for apart in stage[1:]]
        for other in ahead:
            block = after(block, other)
        block = jnp.concatenate([block] + came, axis=axis)
    return block, exchange(block, "dp", stages[-1][1])


def scatter_dp(low, high):
    stages = dp_stages()
    first = exchange(high, "dp", stages[-1][1])
    low, came = low + first.astype(F32), first
    for stage in reversed(stages[:-1]):
        low = low.reshape(low.shape[:2] + (len(stage), -1) + low.shape[-1:])
        total = low[:, :, 0]
        for place, apart in enumerate(stage[1:], 1):
            came = exchange(low[:, :, place].astype(BF16), "dp", apart)
            total = total + came.astype(F32)
        low = total
    return low, first, came


def line_pairs(step):
    last = lax.axis_size("tensor") - 1
    return [(step, step + 1), (last - step, last - step - 1)]


def fold_steps():
    return range(lax.axis_size("tensor") // 2 - 1)


def inward(own):
    total = own
    for step in fold_steps()[:-1]:
        came = lax.ppermute(total, "tensor", line_pairs(step))
        total = (total.astype(F32) + came.astype(F32)).astype(BF16)
    return total


def outward(block, depth):
    for step in reversed(fold_steps()[:-1]):
        came = lax.ppermute(block, "tensor", [(b, a) for a, b in line_pairs(step)])
        block = jnp.where(depth[:, : block.shape[-1]] == step, came, block)
    return block


def swap(into, out, depth):
    if not fold_steps():
        return jnp.zeros_like(into if out is None else out)
    inner = len(fold_steps()) - 1
    pairs = line_pairs(inner)
    back = [(b, a) for a, b in pairs]
    if out is None:
        return lax.ppermute(into, "tensor", pairs)
    if into is None:
        return lax.ppermute(out, "tensor", back)
    block = jnp.where(depth[:, : out.shape[-1]] > inner, out, into)
    return lax.ppermute(block, "tensor", pairs + back)


def across(block):
    half = lax.axis_size("tensor") // 2
    return lax.ppermute(block, "tensor", [(half - 1, half), (half, half - 1)])


def activations(gate, up, grad_hidden):
    sigma = jax.nn.sigmoid(gate)
    silu = gate * sigma
    return jnp.stack(
        [
            silu * up,
            grad_hidden * up * sigma * (1.0 + gate * (1.0 - sigma)),
            grad_hidden * silu,
        ]
    ).astype(BF16)


def shards(tokens, gate_weight, up_weight, down_weight, out_grad):
    mine, width = tokens.shape
    peers = lax.axis_size("dp")
    step = STEP if mine % STEP == 0 else mine
    chunks = mine // step
    half = peers * step // 2
    far, depth, signs, bits, depths = my_row(max(width, gate_weight.shape[1]))
    far = far[:, :width] > 0.5

    square = signs_of(width, depth)
    both = jnp.stack([tokens, out_grad])

    def arrive(turned, ahead=()):
        low, high = gather_dp(turned.reshape(2, -1, 1, step, width), 2, ahead)
        other, own = jnp.where(far, low, high), jnp.where(far, high, low)
        return [part.reshape(2, -1, half, width) for part in (other, own)]

    first = min(2, chunks)
    early = spread(both[:, : first * step])
    late = spread(after(both[:, first * step :], early[1])) if chunks > first else None
    groups = [arrive(rotate(early, signs, square).astype(BF16))]

    def leave(blocks):
        sums = []
        for block in blocks:
            mixed = dot(block[0], down_weight, 1, 0)
            grads = dot(block[1], gate_weight, 1, 1) + dot(block[2], up_weight, 1, 1)
            sums.append(jnp.stack([mixed, grads]))
        sums = jnp.concatenate(sums, axis=1).reshape(2, -1, 2, half, width)
        low = jnp.where(far, sums[:, :, 0], sums[:, :, 1])
        return low, jnp.where(far, sums[:, :, 1], sums[:, :, 0]).astype(BF16)

    def done(i):
        parts = []
        for k in (2 * i + 1, 2 * i):
            inner = depth[:, : outs[k].shape[-1]] > len(fold_steps()) - 1
            parts.append(outward(jnp.where(inner, outs[k], came[k + LAG]), depth))
        return jnp.concatenate(parts, axis=1)

    steps = 2 * chunks
    split, ends = max(chunks - 2, 0), []
    messages, came, crossed, acts, outs = [], [], [], [], []
    for s in range(steps + LAG):
        if s < steps:
            i, which = divmod(s, 2)
            group, place = (groups[0], i) if i < first else (groups[1], i - first)
            x, g = group[which][0, place], group[which][1, place]
            if s > 0:
                other = middle if s == 6 else acts[i - 2] if i > 3 else came[max(s - LAG, 0)] if s > 1 else messages[0][2:]
                x, g = after(x, other), after(g, other)
            parts = [dot(x, gate_weight, 1, 0), dot(x, up_weight, 1, 0), dot(g, down_weight, 1, 1)]
            message = jnp.stack(parts).astype(BF16)
            messages.append(inward(after(message, came[0]) if s == 1 else message))
        if s == steps + LAG - 1 and split > 0:
            low, high = leave([done(i) for i in range(split)])
            first_sums, ahead, _ = scatter_dp(low, high)
            outs[-1] = after(outs[-1], ahead)
        came.append(
            swap(
                messages[s] if s < steps else None,
                outs[s - LAG] if s >= LAG else None,
                depths[s % KINDS],
            )
        )
        if s == 0 and chunks > first:
            tick = exchange(message[2, :step, :width], "dp", 1)
            late[0] = after(late[0], tick)
        if s == 1 and chunks > first:
            groups.append(arrive(rotate(late, signs, square).astype(BF16), [messages[1], middle]))
        if s < steps:
            total = messages[s].astype(F32) + came[s].astype(F32)
            if which == 0:
                middle = total.astype(BF16)
                other_sums = across(middle)
            else:
                gate, up, grad_hidden = total + other_sums.astype(F32)
                acts.append(activations(gate, up, grad_hidden))
                crossed.append(across(acts[i]))
                outs += [acts[i], crossed[i]]
    low, high = leave([done(i) for i in range(split, chunks)])
    sums, _, ahead = scatter_dp(low, high)
    if split > 0:
        first_sums = after(first_sums.reshape(2, -1, width), came[-1])
        block, ahead = rotate_by_halves(first_sums, bits, square, ahead)
        ends.append(block)
    ends.append(rotate(spread(sums.reshape(2, -1, width).astype(BF16)), signs, square))
    ends = jnp.concatenate(ends, axis=1)

    acts = jnp.concatenate([done(i) for i in range(chunks)], axis=1)
    rows = [jnp.stack(group, axis=2).reshape(2, -1, width) for group in groups]
    rows = after(jnp.concatenate(rows, axis=1), high[0, 0, :1])
    late_rows = after(rows[0], ahead.reshape(-1, width)[:1])
    factor = 1.0 / math.sqrt(rows.shape[1])
    return (
        ends[0],
        ends[1],
        (dot(late_rows, acts[1], 0, 0) * factor).astype(BF16),
        (dot(late_rows, acts[2], 0, 0) * factor).astype(BF16),
        (dot(acts[0], rows[1], 0, 0) * factor).astype(BF16),
    )


def solution(mesh):
    return jax.shard_map(
        shards,
        mesh=mesh,
        in_specs=(
            P("dp", "tensor"),
            P("tensor", "dp"),
            P("tensor", "dp"),
            P("dp", "tensor"),
            P("dp", "tensor"),
        ),
        out_specs=(
            P("dp", "tensor"),
            P("dp", "tensor"),
            P("tensor", "dp"),
            P("tensor", "dp"),
            P("dp", "tensor"),
        ),
        check_vma=False,
    )
```

```python
import math

import jax
import jax.numpy as jnp
import numpy as np
from jax import lax
from jax.sharding import PartitionSpec as P

D = 2048
BF16 = jnp.bfloat16
F32 = jnp.float32
STEP = 16
LAG = 3
KINDS = 4


def sylvester(order):
    table = np.ones((1, 1), np.float32)
    while table.shape[0] < order:
        table = np.block([[table, table], [table, -table]])
    return table


def signs_of(order, ahead):
    shape = (order, order)
    common = lax.broadcasted_iota(jnp.int32, shape, 0) & lax.broadcasted_iota(jnp.int32, shape, 1)
    shift = 1
    while shift < order.bit_length():
        shift *= 2
    while shift > 1:
        shift //= 2
        common = common ^ (common >> shift)
    return lax.optimization_barrier(after((1 - 2 * (common & 1)).astype(BF16), ahead))


def dot(left, right, left_dim, right_dim):
    return lax.dot_general(
        left, right, (((left_dim,), (right_dim,)), ((), ())), preferred_element_type=F32
    )


def after(block, other):
    other = other.reshape((-1,) + other.shape[-2:])[0]
    if other.shape[0] < block.shape[-2]:
        other = other[:1]
    other = other[: block.shape[-2]]
    wide = block.shape[-1]
    if other.shape[-1] < wide:
        other = jnp.concatenate([other] * (-(-wide // other.shape[-1])), axis=-1)
    other = other[:, :wide].astype(block.dtype)
    return jnp.where(jnp.isnan(other), other, block)


def my_row(length):
    groups = lax.axis_size("tensor")
    signs = sylvester(groups)
    me = np.arange(groups)
    away = np.minimum(me, groups - 1 - me)
    columns = [me >= groups // 2, away]
    columns += [signs[me, me ^ apart] for apart in range(groups)]
    columns += [1 - 2 * (me >> bit & 1) for bit in range(groups.bit_length() - 1)]
    columns += [away] * KINDS
    table = np.stack(columns, axis=1).astype(np.float32)[:, :, None, None]
    table = jnp.asarray(np.tile(table, (1, 1, 1, length)))
    row = lax.dynamic_index_in_dim(table, lax.axis_index("tensor"), keepdims=False)
    return row[0], row[1], row[2 : 2 + groups], row[2 + groups : -KINDS], row[-KINDS:]


def exchange(block, axis, apart):
    count = lax.axis_size(axis)
    return lax.ppermute(block, axis, [(i, i ^ apart) for i in range(count)])


def spread(block):
    return [block] + [exchange(block, "tensor", k) for k in range(1, lax.axis_size("tensor"))]


def turn(block, square):
    width = block.shape[-1]
    rows = block.reshape(-1, width) * (1.0 / math.sqrt(D))
    high = lax.reduce_precision(rows, 8, 7)
    low = (rows - high).astype(BF16)
    return (dot(high.astype(BF16), square, 1, 0) + dot(low, square, 1, 0)).reshape(block.shape)


def rotate(pieces, signs, square):
    width = pieces[0].shape[-1]
    return turn(sum(piece.astype(F32) * sign[:, :width] for piece, sign in zip(pieces, signs)), square)


def rotate_by_halves(block, bits, square, ahead):
    block = turn(block, square)
    for level, bit in enumerate(bits):
        message = block.astype(BF16)
        message = after(message, ahead) if level else message
        came = exchange(message, "tensor", 1 << level)
        block = block * bit[:, : block.shape[-1]] + came.astype(F32)
    return block, message


def dp_stages():
    bits = [1 << bit for bit in reversed(range(lax.axis_size("dp").bit_length() - 1))]
    stages = []
    while len(bits) > 1:
        high, low, bits = bits[0], bits[1], bits[2:]
        stages.append([0, low, high, high | low])
    if bits:
        stages.append([0, bits[0]])
    return stages


def gather_dp(block, axis, ahead):
    stages = dp_stages()
    for stage in stages[:-1]:
        came = [exchange(block, "dp", apart) for apart in stage[1:]]
        for other in ahead:
            block = after(block, other)
        block = jnp.concatenate([block] + came, axis=axis)
    return block, exchange(block, "dp", stages[-1][1])


def scatter_dp(low, high):
    stages = dp_stages()
    first = exchange(high, "dp", stages[-1][1])
    low, came = low + first.astype(F32), first
    for stage in reversed(stages[:-1]):
        low = low.reshape(low.shape[:2] + (len(stage), -1) + low.shape[-1:])
        total = low[:, :, 0]
        for place, apart in enumerate(stage[1:], 1):
            came = exchange(low[:, :, place].astype(BF16), "dp", apart)
            total = total + came.astype(F32)
        low = total
    return low, first, came


def line_pairs(step):
    last = lax.axis_size("tensor") - 1
    return [(step, step + 1), (last - step, last - step - 1)]


def fold_steps():
    return range(lax.axis_size("tensor") // 2 - 1)


def inward(own):
    total = own
    for step in fold_steps()[:-1]:
        came = lax.ppermute(total, "tensor", line_pairs(step))
        total = (total.astype(F32) + came.astype(F32)).astype(BF16)
    return total


def outward(block, depth):
    for step in reversed(fold_steps()[:-1]):
        came = lax.ppermute(block, "tensor", [(b, a) for a, b in line_pairs(step)])
        block = jnp.where(depth[:, : block.shape[-1]] == step, came, block)
    return block


def swap(into, out, depth):
    if not fold_steps():
        return jnp.zeros_like(into if out is None else out)
    inner = len(fold_steps()) - 1
    pairs = line_pairs(inner)
    back = [(b, a) for a, b in pairs]
    if out is None:
        return lax.ppermute(into, "tensor", pairs)
    if into is None:
        return lax.ppermute(out, "tensor", back)
    block = jnp.where(depth[:, : out.shape[-1]] > inner, out, into)
    return lax.ppermute(block, "tensor", pairs + back)


def across(block):
    half = lax.axis_size("tensor") // 2
    return lax.ppermute(block, "tensor", [(half - 1, half), (half, half - 1)])


def activations(gate, up, grad_hidden):
    sigma = jax.nn.sigmoid(gate)
    silu = gate * sigma
    return jnp.stack(
        [
            silu * up,
            grad_hidden * up * sigma * (1.0 + gate * (1.0 - sigma)),
            grad_hidden * silu,
        ]
    ).astype(BF16)


def shards(tokens, gate_weight, up_weight, down_weight, out_grad):
    mine, width = tokens.shape
    peers = lax.axis_size("dp")
    step = STEP if mine % STEP == 0 else mine
    chunks = mine // step
    half = peers * step // 2
    far, depth, signs, bits, depths = my_row(max(width, gate_weight.shape[1]))
    far = far[:, :width] > 0.5

    square = signs_of(width, depth)
    both = jnp.stack([tokens, out_grad])

    def arrive(turned, ahead=()):
        low, high = gather_dp(turned.reshape(2, -1, 1, step, width), 2, ahead)
        other, own = jnp.where(far, low, high), jnp.where(far, high, low)
        return [part.reshape(2, -1, half, width) for part in (other, own)]

    first = min(2, chunks)
    early = spread(both[:, : first * step])
    late = spread(after(both[:, first * step :], early[1])) if chunks > first else None
    groups = [arrive(rotate(early, signs, square).astype(BF16))]

    def leave(blocks):
        sums = []
        for block in blocks:
            mixed = dot(block[0], down_weight, 1, 0)
            grads = dot(block[1], gate_weight, 1, 1) + dot(block[2], up_weight, 1, 1)
            sums.append(jnp.stack([mixed, grads]))
        sums = jnp.concatenate(sums, axis=1).reshape(2, -1, 2, half, width)
        low = jnp.where(far, sums[:, :, 0], sums[:, :, 1])
        return low, jnp.where(far, sums[:, :, 1], sums[:, :, 0]).astype(BF16)

    def done(i):
        parts = []
        for k in (2 * i + 1, 2 * i):
            inner = depth[:, : outs[k].shape[-1]] > len(fold_steps()) - 1
            parts.append(outward(jnp.where(inner, outs[k], came[k + LAG]), depth))
        return jnp.concatenate(parts, axis=1)

    steps = 2 * chunks
    split, ends = max(chunks - 2, 0), []
    messages, came, mids, crossed, acts, outs = [], [], [], [], [], []
    for s in range(steps + LAG):
        if s < steps:
            i, which = divmod(s, 2)
            group, place = (groups[0], i) if i < first else (groups[1], i - first)
            x, g = group[which][0, place], group[which][1, place]
            if s > 0:
                other = middle if s == 6 else mids[i - 2] if i > 3 else came[max(s - LAG, 0)] if s > 1 else messages[0][2:]
                x, g = after(x, other), after(g, other)
            parts = [dot(x, gate_weight, 1, 0), dot(x, up_weight, 1, 0), dot(g, down_weight, 1, 1)]
            message = jnp.stack(parts).astype(BF16)
            messages.append(inward(after(message, came[0]) if s == 1 else message))
        if s == steps + LAG - 1 and split > 0:
            low, high = leave([done(i) for i in range(split)])
            first_sums, ahead, _ = scatter_dp(low, high)
            outs[-1] = after(outs[-1], ahead)
        came.append(
            swap(
                messages[s] if s < steps else None,
                outs[s - LAG] if s >= LAG else None,
                depths[s % KINDS],
            )
        )
        if s == 0 and chunks > first:
            tick = exchange(message[2, :step, :width], "dp", 1)
            late[0] = after(late[0], tick)
        if s == 1 and chunks > first:
            groups.append(arrive(rotate(late, signs, square).astype(BF16), [messages[1], middle]))
        if s < steps:
            total = messages[s].astype(F32) + came[s].astype(F32)
            if which == 0:
                middle = total.astype(BF16)
                mids.append(middle)
                other_sums = across(middle)
            else:
                gate, up, grad_hidden = total + other_sums.astype(F32)
                acts.append(activations(gate, up, grad_hidden))
                crossed.append(across(acts[i]))
                outs += [acts[i], crossed[i]]
    low, high = leave([done(i) for i in range(split, chunks)])
    sums, _, ahead = scatter_dp(low, high)
    if split > 0:
        first_sums = after(first_sums.reshape(2, -1, width), came[-1])
        block, ahead = rotate_by_halves(first_sums, bits, square, ahead)
        ends.append(block)
    ends.append(rotate(spread(sums.reshape(2, -1, width).astype(BF16)), signs, square))
    ends = jnp.concatenate(ends, axis=1)

    acts = jnp.concatenate([done(i) for i in range(chunks)], axis=1)
    rows = [jnp.stack(group, axis=2).reshape(2, -1, width) for group in groups]
    rows = after(jnp.concatenate(rows, axis=1), high[0, 0, :1])
    late_rows = after(rows[0], ahead.reshape(-1, width)[:1])
    factor = 1.0 / math.sqrt(rows.shape[1])
    return (
        ends[0],
        ends[1],
        (dot(late_rows, acts[1], 0, 0) * factor).astype(BF16),
        (dot(late_rows, acts[2], 0, 0) * factor).astype(BF16),
        (dot(acts[0], rows[1], 0, 0) * factor).astype(BF16),
    )


def solution(mesh):
    return jax.shard_map(
        shards,
        mesh=mesh,
        in_specs=(
            P("dp", "tensor"),
            P("tensor", "dp"),
            P("tensor", "dp"),
            P("dp", "tensor"),
            P("dp", "tensor"),
        ),
        out_specs=(
            P("dp", "tensor"),
            P("dp", "tensor"),
            P("tensor", "dp"),
            P("tensor", "dp"),
            P("dp", "tensor"),
        ),
        check_vma=False,
    )
```
